32 devices in a mesh: pole: 2 (over y), prow: 8 (over z, x), pcol: 2 (over core).
Axes of the slice: x: 2, y: 2, z: 4, core: 2. Of those that a mesh axis runs over, the one named last changes fastest.
Arguments:
- anc_inverse: bfloat16 [4, 8, 2, 48, 768], P('pole', None, 'pcol', None, 'prow'), parts along dimension 0, may hold values from -6 to 6
- panels: bfloat16 [6, 2, 768, 128], P('pole', None, ('prow', 'pcol')), parts along dimension 0, may hold values from -0.3125 to 0.3125
- diag_inverse: bfloat16 [6, 2, 128, 128], P('pole'), parts along dimension 0, may hold values from -3 to 3
- structure: int32 [3, 6], replicated, may hold values 0 or 1
Outputs:
- inverse_columns: bfloat16 [6, 2, 768, 128], P('pole', None, ('prow', 'pcol')), parts along dimension 0
- inverse_diag: float32 [6, 2, 128, 128], P('pole'), parts along dimension 0
The draws below stay inside these ranges and needn't reach their ends.
There are 2 independent parts, one for each index of `pole`. The reference program is written for one: setup_inputs(seed, part) draws one part's arguments, and reference() takes and returns one part's arrays. A program takes and returns all parts, laid end to end along the dimension named above; an argument that names none is the same for every part. Nothing has to cross between parts.
All inputs are finite; a program needn't handle non-finite values.
Results may differ from the reference program's by a relative error of at most 0.0027.
Values may be sent and summed in bfloat16 or wider, within the bound.
No kernel may reach another device: no remote copies, remote signals or barrier semaphores. Data moves between devices by JAX's collectives and lax.ppermute only.
A program may use at most 64 MiB of HBM per device.

```python
import jax
import jax.numpy as jnp
from jax import lax

W = 128
NK = 3
RH = 48
ROWGROUPS = 8
ANC = 768
NBLK = 6


def place_ends(drawn, rng, least, top_value):
    longest = drawn.shape.index(max(drawn.shape))
    spots = []
    for shift in (0, 1):
        where = [jax.random.randint(jax.random.fold_in(rng, axis), (), 0, length) for axis, length in enumerate(drawn.shape)]
        where[longest] = (where[longest] + shift) % drawn.shape[longest]
        spots.append(tuple(where))
    return drawn.at[spots[0]].set(least).at[spots[1]].set(top_value)


def block_scale(stream_key, shape, pieces, smallest, largest):
    def one(dim, parts):
        draws = jax.random.uniform(jax.random.fold_in(jax.random.fold_in(stream_key, 6), dim), (parts,), jnp.float32, smallest / len(pieces), largest / len(pieces))
        return jnp.repeat(jnp.exp(draws), shape[dim] // parts).reshape((-1,) + (1,) * (len(shape) - dim - 1))

    loudness = one(*pieces[0])
    for cut in pieces[1:]:
        loudness = loudness * one(*cut)
    return loudness


def gaussian(stream_key, dims, width, limit, pieces=(), held_as=jnp.bfloat16):
    level = block_scale(stream_key, dims, pieces, -0.22, 0.18) if pieces else 1.0
    entries = jax.random.normal(stream_key, dims, jnp.float32) * width * level
    return jnp.minimum(jnp.maximum(entries, -limit), limit).astype(held_as)


def setup_inputs(seed: int = 0, part: int = 0) -> dict:
    seeds = jax.random.split(jax.random.key(seed), 5)
    part_splits = jax.random.split(jax.random.fold_in(seeds[4], part), 5)
    anc_inverse = gaussian(part_splits[0], (2, ROWGROUPS, 2, RH, ANC), 1.0, 6.0, ((2, 2), (4, 8)))
    panels = gaussian(part_splits[1], (NK, 2, ANC, W), (ANC // 2) ** -0.5, 0.3125, ((2, 16),))
    diag_inverse = gaussian(part_splits[2], (NK, 2, W, W), 0.5, 3.0)
    structure = place_ends((jax.random.randint(seeds[3], (NK, NBLK), 0, 2) < 1).astype(jnp.int32), jax.random.fold_in(seeds[3], 1), 0, 1)
    return {"anc_inverse": anc_inverse, "panels": panels, "diag_inverse": diag_inverse, "structure": structure}


def contract_rows(left, right):
    return lax.dot_general(left, right, (((0,), (0,)), ((), ())), preferred_element_type=jnp.float32)


def complex_product(left, right):
    real_part = contract_rows(left[0], right[0]) - contract_rows(left[1], right[1])
    imag_part = contract_rows(left[0], right[1]) + contract_rows(left[1], right[0])
    return jnp.stack([real_part, imag_part])


def reference(anc_inverse, panels, diag_inverse, structure):
    matrix = anc_inverse.reshape(2, ANC, ANC)
    block_of_row = jnp.arange(ANC, dtype=jnp.int32) // W
    row_mask = structure[:, block_of_row]
    columns_out = []
    diags = []
    for node in range(NK):
        keep_float = row_mask[node].astype(jnp.float32)[None, :, None]
        masked = panels[node] * row_mask[node].astype(panels.dtype)[None, :, None]
        product = complex_product(matrix, masked)
        column = (-(product * keep_float)).astype(panels.dtype)
        diag = diag_inverse[node].astype(jnp.float32) - complex_product(masked, column)
        columns_out.append(column)
        diags.append(diag)
    return jnp.stack(columns_out), jnp.stack(diags)
```

```python
import jax
import jax.numpy as jnp
from jax import lax
from jax.sharding import PartitionSpec as P

AXES = ("prow", "pcol")


def swap(value, rows, cols, mask0, mask1):
    pairs = []
    for row in range(rows):
        for col in range(cols):
            mask = mask0 if col == 0 else mask1
            pairs.append((row * cols + col, (row ^ mask) * cols + col))
    return lax.ppermute(value, AXES, pairs)


def swap_core(value):
    return lax.ppermute(value, "pcol", [(0, 1), (1, 0)])


def gather(block, rows, cols, row_index, col_index):
    half = rows // 2
    here = row_index // 2
    held = jnp.zeros((half,) + block.shape, block.dtype)
    masks = [(2, 4), (4, 2), (6, 6)]
    arrived = [swap(block, rows, cols, m0, m1) for m0, m1 in masks]
    held = lax.dynamic_update_index_in_dim(held, block, here, 0)
    for (m0, m1), value in zip(masks, arrived):
        step = jnp.where(col_index == 0, m0, m1) // 2
        held = lax.dynamic_update_index_in_dim(held, value, here ^ step, 0)
    size = 8
    while size < rows:
        count = size // 2
        start = (here // count) * count
        own = lax.dynamic_slice_in_dim(held, start, count, 0)
        other = swap(own, rows, cols, size, size)
        held = lax.dynamic_update_slice_in_dim(held, other, start ^ count, 0)
        size *= 2
    return held, swap(held, rows, cols, 1, 1)


def contract(left, right):
    both = lax.dot_general(
        left, right, (((0, 2), (0, 3)), ((), ())), preferred_element_type=jnp.float32
    )
    real = both[0, :, :, 0] - both[1, :, :, 1]
    imag = both[0, :, :, 1] + both[1, :, :, 0]
    return jnp.stack([real, imag]).transpose(2, 0, 1, 3)


def contract_nodes(left, right):
    both = lax.dot_general(
        left, right, (((0, 3), (0, 3)), ((1,), (1,))), preferred_element_type=jnp.float32
    )
    real = both[:, 0, :, 0] - both[:, 1, :, 1]
    imag = both[:, 0, :, 1] + both[:, 1, :, 0]
    return jnp.stack([real, imag], axis=1)


def solution(mesh):
    rows, cols = mesh.shape["prow"], mesh.shape["pcol"]

    def local(anc_inverse, panels, diag_inverse, structure):
        supernodes, _, rows_half, width = panels.shape
        groups = anc_inverse.shape[1]
        rows_dev = anc_inverse.shape[4]
        row_index = lax.axis_index("prow")
        col_index = lax.axis_index("pcol")
        blocks = structure.shape[1]
        local_rows = (
            row_index * rows_dev + col_index * rows_half + jnp.arange(rows_half, dtype=jnp.int32)
        )
        hits = local_rows[:, None] // width == jnp.arange(blocks, dtype=jnp.int32)[None, :]
        keep = jnp.sum(jnp.where(hits[None], structure[:, None, :], 0), axis=2)
        masked = panels * keep.astype(jnp.bfloat16)[:, None, :, None]

        matrix = anc_inverse.reshape(2, groups // 2, 2, rows_half, rows_dev)
        parity = row_index % 2
        own = lax.dynamic_index_in_dim(matrix, parity, 2, False).swapaxes(0, 1)
        far = lax.dynamic_index_in_dim(matrix, 1 - parity, 2, False).swapaxes(0, 1)

        m_own, m_far = gather(masked, rows, cols, row_index, col_index)
        partial = contract(own, m_own) + contract(far, m_far)
        halves = partial.reshape(supernodes, 2, cols, rows_half, width)
        mine = lax.dynamic_index_in_dim(halves, col_index, 2, False)
        theirs = lax.dynamic_index_in_dim(halves, 1 - col_index, 2, False)
        product = mine + swap_core(theirs)
        column = (-(product * keep.astype(jnp.float32)[:, None, :, None])).astype(jnp.bfloat16)

        c_own, c_far = gather(column, rows, cols, row_index, col_index)
        diag = contract_nodes(m_own, c_own) + contract_nodes(m_far, c_far)
        diag = diag + swap_core(diag)
        return column, diag_inverse.astype(jnp.float32) - diag

    in_specs = (
        P("pole", None, "pcol", None, "prow"),
        P("pole", None, ("prow", "pcol"), None),
        P("pole", None, None, None),
        P(),
    )
    out_specs = (P("pole", None, ("prow", "pcol"), None), P("pole", None, None, None))
    return jax.shard_map(local, mesh=mesh, in_specs=in_specs, out_specs=out_specs, check_vma=False)
```

```python
import jax
import jax.numpy as jnp
from jax import lax
from jax.sharding import PartitionSpec as P

AXES = ("prow", "pcol")
MASKS = ((2, 4), (4, 2), (6, 6))


def swap(value, rows, cols, mask0, mask1):
    pairs = []
    for row in range(rows):
        for col in range(cols):
            mask = mask0 if col == 0 else mask1
            pairs.append((row * cols + col, (row ^ mask) * cols + col))
    return lax.ppermute(value, AXES, pairs)


def swap_core(value):
    return lax.ppermute(value, "pcol", [(0, 1), (1, 0)])


def gather(block, rows, cols, here, col_index):
    held = jnp.zeros((rows // 2,) + block.shape, block.dtype)
    held = lax.dynamic_update_index_in_dim(held, block, here, 0)
    for mask0, mask1 in MASKS:
        value = swap(block, rows, cols, mask0, mask1)
        step = jnp.where(col_index == 0, mask0, mask1) // 2
        held = lax.dynamic_update_index_in_dim(held, value, here ^ step, 0)
    size = 8
    while size < rows:
        count = size // 2
        start = (here // count) * count
        own = lax.dynamic_slice_in_dim(held, start, count, 0)
        other = swap(own, rows, cols, size, size)
        held = lax.dynamic_update_slice_in_dim(held, other, start ^ count, 0)
        size *= 2
    return held


def total(block, rows, cols):
    sent = block.astype(jnp.bfloat16)
    first, second, third = [
        swap(sent, rows, cols, mask0, mask1).astype(jnp.float32) for mask0, mask1 in MASKS
    ]
    result = (sent.astype(jnp.float32) + first) + (second + third)
    size = 8
    while size < rows:
        result = result + swap(result, rows, cols, size, size)
        size *= 2
    return result


def pack(value, side, half):
    part = lax.dynamic_slice_in_dim(value, side * half, half, value.ndim - 1)
    return jnp.concatenate([part[..., 0, :, :], part[..., 1, :, :]], axis=-1)


def turned(value, half):
    return jnp.concatenate([-value[..., half:], value[..., :half]], axis=-1)


def solution(mesh):
    rows, cols = mesh.shape["prow"], mesh.shape["pcol"]

    def local(anc_inverse, panels, diag_inverse, structure):
        supernodes, _, rows_half, width = panels.shape
        half = width // 2
        groups = anc_inverse.shape[1]
        rows_dev = anc_inverse.shape[4]
        row_index = lax.axis_index("prow")
        col_index = lax.axis_index("pcol")
        here, parity = row_index // 2, row_index % 2
        blocks = structure.shape[1]

        panels_far = swap(panels, rows, cols, 1, 1)
        matrix_far = swap(anc_inverse, rows, cols, 1, 1)

        def keep_of(row):
            local_rows = row * rows_dev + col_index * rows_half + jnp.arange(rows_half, dtype=jnp.int32)
            hits = local_rows[:, None] // width == jnp.arange(blocks, dtype=jnp.int32)[None, :]
            return jnp.sum(jnp.where(hits[None], structure[:, None, :], 0), axis=2)

        keep = jnp.stack([keep_of(row_index), keep_of(row_index ^ 1)])
        masked = jnp.stack([panels, panels_far]) * keep.astype(jnp.bfloat16)[:, :, None, :, None]

        block = pack(masked, parity, half)
        held = gather(block, rows, cols, here, col_index)

        def ordered(matrix):
            cut = matrix.reshape(2, groups // 2, 2, rows_half, rows_dev).transpose(1, 2, 0, 3, 4)
            return jnp.where(parity == 0, cut, cut[:, ::-1])

        left = jnp.stack([ordered(anc_inverse), ordered(matrix_far)], axis=4)
        right = jnp.stack([held, turned(held, half)], axis=2)
        partial = lax.dot_general(
            left, right, (((0, 1, 2, 3), (0, 1, 2, 4)), ((), ())), preferred_element_type=jnp.float32
        )
        halves = partial.reshape(2, cols, rows_half, supernodes, 2 * half)
        mine = lax.dynamic_index_in_dim(halves, col_index, 1, False)
        theirs = lax.dynamic_index_in_dim(halves, 1 - col_index, 1, False)
        product = mine + swap_core(theirs)
        keep_float = keep.astype(jnp.float32).transpose(0, 2, 1)[..., None]
        column = (-(product * keep_float)).astype(jnp.bfloat16)

        left = masked.transpose(0, 2, 3, 1, 4)
        right = jnp.stack([column, turned(column, half)], axis=1)
        diag = lax.dot_general(
            left, right, (((0, 1, 2), (0, 1, 2)), ((3,), (3,))), preferred_element_type=jnp.float32
        )
        cut = diag.reshape(supernodes, cols, width // cols, 2 * half)
        mine = lax.dynamic_index_in_dim(cut, col_index, 1, False)
        theirs = lax.dynamic_index_in_dim(cut, 1 - col_index, 1, False)
        mine = mine + swap_core(theirs)
        mine = total(mine, rows, cols)

        def whole(near, far, axis):
            low = jnp.where(parity == 0, near, far)
            high = jnp.where(parity == 0, far, near)
            real = jnp.concatenate([low[..., :half], high[..., :half]], axis=-1)
            imag = jnp.concatenate([low[..., half:], high[..., half:]], axis=-1)
            return jnp.stack([real, imag], axis=axis)

        diag_half = whole(mine, swap(mine, rows, cols, 1, 1), 1)
        other = swap_core(diag_half)
        low = jnp.where(col_index == 0, diag_half, other)
        high = jnp.where(col_index == 0, other, diag_half)
        diag = jnp.concatenate([low, high], axis=2)

        column_far = swap(column[1], rows, cols, 1, 1)
        columns = whole(column[0], column_far, 0).transpose(2, 0, 1, 3)
        return columns, diag_inverse.astype(jnp.float32) - diag

    in_specs = (
        P("pole", None, "pcol", None, "prow"),
        P("pole", None, ("prow", "pcol"), None),
        P("pole", None, None, None),
        P(),
    )
    out_specs = (P("pole", None, ("prow", "pcol"), None), P("pole", None, None, None))
    return jax.shard_map(local, mesh=mesh, in_specs=in_specs, out_specs=out_specs, check_vma=False)
```

```python
import functools

import jax
import jax.numpy as jnp
from jax import lax
from jax.experimental import pallas as pl
from jax.experimental.layout import Layout, with_layout_constraint
from jax.experimental.pallas import tpu as pltpu
from jax.sharding import PartitionSpec as P

AXES = ("prow", "pcol")
MASKS = ((2, 4), (4, 2), (6, 6))
MASKS_SUM = ((2, 2), (4, 4), (6, 6))
VMEM = pl.BlockSpec(memory_space=pltpu.VMEM)


def swap(value, rows, cols, mask0, mask1):
    pairs = []
    for row in range(rows):
        for col in range(cols):
            mask = mask0 if col == 0 else mask1
            pairs.append((row * cols + col, (row ^ mask) * cols + col))
    return lax.ppermute(value, AXES, pairs)


def swap_core(value):
    return lax.ppermute(value, "pcol", [(0, 1), (1, 0)])


def after(value, *others):
    return lax.optimization_barrier((value,) + others)[0]


def plain(value):
    return with_layout_constraint(value, Layout(tuple(range(value.ndim))))


def call(kernel, outs, operands, scratch=()):
    shapes = [jax.ShapeDtypeStruct(shape, dtype) for shape, dtype in outs]
    size = sum(v.size * v.dtype.itemsize for v in list(operands) + shapes)
    return pl.pallas_call(
        kernel,
        out_shape=shapes,
        in_specs=[VMEM] * len(operands),
        out_specs=[VMEM] * len(shapes),
        scratch_shapes=list(scratch),
        compiler_params=pltpu.CompilerParams(vmem_limit_bytes=2 * size + (4 << 20)),
    )(*operands)


def keep_rows(structure, node, start, count, width):
    blocks = structure.shape[1]
    row = start + lax.broadcasted_iota(jnp.int32, (count, blocks), 0)
    hit = row // width == lax.broadcasted_iota(jnp.int32, (count, blocks), 1)
    table = structure[node : node + 1, :].astype(jnp.float32)
    return jnp.sum(jnp.where(hit, table, 0.0), axis=1, keepdims=True)


def swap_halves(value):
    half = value.shape[-1] // 2
    return jnp.concatenate([value[:, half:], value[:, :half]], axis=-1)


def turned(value):
    lane = lax.broadcasted_iota(jnp.int32, value.shape, 1)
    other = swap_halves(value)
    return jnp.where(lane < value.shape[-1] // 2, -other, other)


def pick_kernel(structure, panels, panels_far, block):
    supernodes, _, rows_half, width = panels.shape
    row_index, col_index = lax.axis_index("prow"), lax.axis_index("pcol")
    parity = row_index % 2
    lane = lax.broadcasted_iota(jnp.int32, (rows_half, width), 1)
    low = lane < width // 2
    for far, source in ((0, panels), (1, panels_far)):
        start = ((row_index ^ far) * 2 + col_index) * rows_half
        for node in range(supernodes):
            keep = keep_rows(structure, node, start, rows_half, width)
            real = source[node, 0].astype(jnp.float32)
            imag = source[node, 1].astype(jnp.float32)
            left = jnp.where(low, real, swap_halves(imag))
            right = jnp.where(low, swap_halves(real), imag)
            value = jnp.where(parity == 0, left, right) * keep
            block[parity ^ far, :, node * width : (node + 1) * width] = value.astype(jnp.bfloat16)


def product_kernel(width, near, far, held, out, held_turned):
    count, _, rows_half, lanes = held.shape
    supernodes = lanes // width

    def turn(index, _):
        for x in range(2):
            for node in range(supernodes):
                part = slice(node * width, (node + 1) * width)
                value = held[index, x, :, part].astype(jnp.float32)
                held_turned[index, x, :, part] = turned(value).astype(jnp.bfloat16)
        return _

    if count <= 4:
        for index in range(count):
            turn(index, 0)
    else:
        lax.fori_loop(0, count, turn, 0)
    depth = count * 2 * rows_half
    real = held[...].reshape(depth, lanes)
    imag = held_turned[...].reshape(depth, lanes)
    for far_or, left in ((0, near), (1, far)):
        out[far_or] = jnp.dot(
            left[:, :depth], real, preferred_element_type=jnp.float32
        ) + jnp.dot(left[:, depth:], imag, preferred_element_type=jnp.float32)


def diagonal_kernel(structure, mine, theirs, panels, panels_far, panels_core, panels_far_core, own, far, diag, left, right, full):
    supernodes, _, rows_half, width = panels.shape
    row_index, col_index = lax.axis_index("prow"), lax.axis_index("pcol")
    rows_dev = 2 * rows_half
    for far_or, (same, cross) in ((0, (panels, panels_core)), (1, (panels_far, panels_far_core))):
        start = (row_index ^ far_or) * rows_dev
        for node in range(supernodes):
            for part in range(2):
                left[node, far_or, part, col_index] = same[node, part]
                left[node, far_or, part, 1 - col_index] = cross[node, part]
            lanes = slice(node * width, (node + 1) * width)
            keep = keep_rows(structure, node, start, rows_dev, width)
            value = -((mine[far_or, :, lanes] + theirs[far_or, :, lanes]) * keep)
            value = value.astype(jnp.bfloat16).astype(jnp.float32)
            column = value.astype(jnp.bfloat16).reshape(2, rows_half, width)
            right[node, far_or, 0] = column
            right[node, far_or, 1] = turned(value).astype(jnp.bfloat16).reshape(2, rows_half, width)
            out = own if far_or == 0 else far
            out[node] = right[node, far_or, 0, col_index]
    depth = 4 * rows_dev
    for node in range(supernodes):
        full[node] = lax.dot_general(
            left[node].reshape(depth, width),
            right[node].reshape(depth, width),
            (((0,), (0,)), ((), ())),
            preferred_element_type=jnp.float32,
        )
    half = width // 2
    diag[...] = full[:, pl.ds(pl.multiple_of(col_index * half, half), half), :]


def unpack(near, far):
    parity = lax.axis_index("prow") % 2
    low = jnp.where(parity == 0, near, far)
    high = jnp.where(parity == 0, far, near)
    first = lax.broadcasted_iota(jnp.int32, near.shape, 1) < near.shape[1] // 2
    return jnp.where(first, low, swap_halves(high)), jnp.where(first, swap_halves(low), high)


def sum_kernel(terms, columns, packet):
    first, second, third, fourth = [term[...].astype(jnp.float32) for term in terms]
    value = (first + second) + (third + fourth)
    high = value.astype(jnp.bfloat16)
    rows = value.shape[0]
    packet[:rows] = high
    packet[rows : 2 * rows] = (value - high.astype(jnp.float32)).astype(jnp.bfloat16)
    packet[2 * rows :] = columns[...]


def columns_kernel(own, other, out):
    supernodes, _, rows_half, width = out.shape
    for node in range(supernodes):
        rows = slice(node * rows_half, (node + 1) * rows_half)
        real, imag = unpack(
            own[rows].astype(jnp.float32),
            other[rows].astype(jnp.float32),
        )
        out[node, 0] = real.astype(jnp.bfloat16)
        out[node, 1] = imag.astype(jnp.bfloat16)


def final_kernel(diag_inverse, mine, far, mine_core, far_core, out):
    supernodes, _, width, _ = out.shape
    half = width // 2
    col_index = lax.axis_index("pcol")

    def value(ref, node):
        first, second = node * half, (supernodes + node) * half
        return ref[first : first + half].astype(jnp.float32) + ref[second : second + half].astype(jnp.float32)

    for node in range(supernodes):
        for col, near_ref, far_ref in ((col_index, mine, far), (1 - col_index, mine_core, far_core)):
            rows = pl.ds(pl.multiple_of(col * half, half), half)
            real, imag = unpack(value(near_ref, node), value(far_ref, node))
            out[node, 0, rows] = diag_inverse[node, 0, rows].astype(jnp.float32) - real
            out[node, 1, rows] = diag_inverse[node, 1, rows].astype(jnp.float32) - imag


def solution(mesh):
    rows, cols = mesh.shape["prow"], mesh.shape["pcol"]

    def local(anc_inverse, panels, diag_inverse, structure):
        supernodes, _, rows_half, width = panels.shape
        half = width // 2
        groups = anc_inverse.shape[1]
        rows_dev = anc_inverse.shape[4]
        lanes = supernodes * width
        row_index = lax.axis_index("prow")
        col_index = lax.axis_index("pcol")
        here = row_index // 2
        bf16, f32 = jnp.bfloat16, jnp.float32

        panels = plain(panels)
        panels_far = plain(swap(panels, rows, cols, 1, 1))
        near = anc_inverse.reshape(2 * groups * rows_half, rows_dev).T
        far = swap(near, rows, cols, 1, 1)

        (block,) = call(
            pick_kernel, [((2, rows_half, lanes), bf16)], [structure, panels, panels_far]
        )
        held = jnp.zeros((rows // 2,) + block.shape, bf16)
        held = lax.dynamic_update_index_in_dim(held, block, here, 0)
        arrived = [swap(block, rows, cols, mask0, mask1) for mask0, mask1 in MASKS]
        panels_core = swap_core(panels)
        panels_far_core = swap_core(panels_far)
        for (mask0, mask1), value in zip(MASKS, arrived):
            step = jnp.where(col_index == 0, mask0, mask1) // 2
            held = lax.dynamic_update_index_in_dim(held, value, here ^ step, 0)
        size = 8
        while size < rows:
            count = size // 2
            start = (here // count) * count
            own = lax.dynamic_slice_in_dim(held, start, count, 0)
            other = swap(own, rows, cols, size, size)
            held = lax.dynamic_update_slice_in_dim(held, other, start ^ count, 0)
            size *= 2

        held = after(held, panels_core, panels_far_core)
        (partial,) = call(
            functools.partial(product_kernel, width),
            [((2, rows_dev, lanes), f32)],
            [near, far, held],
            [pltpu.VMEM(held.shape, bf16)],
        )
        pieces = (supernodes, 2, 2, cols, rows_half, width)
        own, send, diag = call(
            diagonal_kernel,
            [((supernodes, rows_half, width), bf16)] * 2 + [((supernodes, half, width), f32)],
            [structure, partial, swap_core(partial), panels, panels_far, panels_core, panels_far_core],
            [pltpu.VMEM(pieces, bf16), pltpu.VMEM(pieces, bf16), pltpu.VMEM((supernodes, width, width), f32)],
        )
        count = supernodes * half
        term = diag.astype(bf16).reshape(count, width)
        terms = [term] + [swap(term, rows, cols, mask0, mask1) for mask0, mask1 in MASKS_SUM]
        size = 8
        while size < rows:
            first, second, third, fourth = [t.astype(f32) for t in terms]
            term = (first + second) + (third + fourth)
            other = swap(term, rows, cols, size, size)
            terms = [term, other, jnp.zeros_like(term), jnp.zeros_like(term)]
            size *= 2
        columns_rows = supernodes * rows_half
        (packet,) = call(
            lambda *refs: sum_kernel(refs[:4], refs[4], refs[5]),
            [((2 * count + columns_rows, width), bf16)],
            terms + [send.reshape(columns_rows, width)],
        )
        other = swap(packet, rows, cols, 1, 1)
        mine, far = packet[: 2 * count], other[: 2 * count]
        (columns,) = call(
            columns_kernel,
            [((supernodes, 2, rows_half, width), bf16)],
            [own.reshape(columns_rows, width), other[2 * count :]],
        )
        (diag,) = call(
            final_kernel,
            [((supernodes, 2, width, width), f32)],
            [diag_inverse, mine, far, swap_core(mine), swap_core(far)],
        )
        return columns, diag

    in_specs = (
        P("pole", None, "pcol", None, "prow"),
        P("pole", None, ("prow", "pcol"), None),
        P("pole", None, None, None),
        P(),
    )
    out_specs = (P("pole", None, ("prow", "pcol"), None), P("pole", None, None, None))
    return jax.shard_map(local, mesh=mesh, in_specs=in_specs, out_specs=out_specs, check_vma=False)
```

```python
import functools
import math

import jax
import jax.numpy as jnp
from jax import lax
from jax.experimental import pallas as pl
from jax.experimental.layout import Layout, with_layout_constraint
from jax.experimental.pallas import tpu as pltpu
from jax.sharding import PartitionSpec as P

AXES = ("prow", "pcol")
MASKS = ((6, 6), (2, 4), (4, 2))
MASKS_SUM = ((2, 2), (4, 4), (6, 6))
VMEM = pl.BlockSpec(memory_space=pltpu.VMEM)


def swap(value, rows, cols, mask0, mask1):
    pairs = []
    for row in range(rows):
        for col in range(cols):
            mask = mask0 if col == 0 else mask1
            pairs.append((row * cols + col, (row ^ mask) * cols + col))
    return lax.ppermute(value, AXES, pairs)


def swap_core(value):
    return lax.ppermute(value, "pcol", [(0, 1), (1, 0)])


def after(value, *others):
    return lax.optimization_barrier((value,) + others)[0]


def plain(value):
    return with_layout_constraint(value, Layout(tuple(range(value.ndim))))


def call(kernel, outs, operands, scratch=()):
    shapes = [jax.ShapeDtypeStruct(shape, dtype) for shape, dtype in outs]
    size = sum(v.size * v.dtype.itemsize for v in list(operands) + shapes)
    return pl.pallas_call(
        kernel,
        out_shape=shapes,
        in_specs=[VMEM] * len(operands),
        out_specs=[VMEM] * len(shapes),
        scratch_shapes=list(scratch),
        compiler_params=pltpu.CompilerParams(vmem_limit_bytes=2 * size + (4 << 20)),
    )(*operands)


def keep_rows(structure, node, start, count, width):
    blocks = structure.shape[1]
    row = start + lax.broadcasted_iota(jnp.int32, (count, blocks), 0)
    hit = row // width == lax.broadcasted_iota(jnp.int32, (count, blocks), 1)
    table = structure[node : node + 1, :].astype(jnp.float32)
    return jnp.sum(jnp.where(hit, table, 0.0), axis=1, keepdims=True)


def swap_halves(value):
    half = value.shape[-1] // 2
    return jnp.concatenate([value[:, half:], value[:, :half]], axis=-1)


def turned(value):
    lane = lax.broadcasted_iota(jnp.int32, value.shape, 1)
    other = swap_halves(value)
    return jnp.where(lane < value.shape[-1] // 2, -other, other)


def pick_kernel(structure, panels, panels_far, block):
    supernodes, _, rows_half, width = panels.shape
    row_index, col_index = lax.axis_index("prow"), lax.axis_index("pcol")
    parity = row_index % 2
    lane = lax.broadcasted_iota(jnp.int32, (rows_half, width), 1)
    low = lane < width // 2
    for far, source in ((0, panels), (1, panels_far)):
        start = ((row_index ^ far) * 2 + col_index) * rows_half
        for node in range(supernodes):
            keep = keep_rows(structure, node, start, rows_half, width)
            real = source[node, 0].astype(jnp.float32)
            imag = source[node, 1].astype(jnp.float32)
            left = jnp.where(low, real, swap_halves(imag))
            right = jnp.where(low, swap_halves(real), imag)
            value = jnp.where(parity == 0, left, right) * keep
            block[parity ^ far, :, node * width : (node + 1) * width] = value.astype(jnp.bfloat16)


def product_kernel(width, near, far, held, out, held_turned):
    count, _, rows_half, lanes = held.shape
    supernodes = lanes // width

    def turn(index, _):
        for x in range(2):
            for node in range(supernodes):
                part = slice(node * width, (node + 1) * width)
                value = held[index, x, :, part].astype(jnp.float32)
                held_turned[index, x, :, part] = turned(value).astype(jnp.bfloat16)
        return _

    if count <= 4:
        for index in range(count):
            turn(index, 0)
    else:
        lax.fori_loop(0, count, turn, 0)
    depth = count * 2 * rows_half
    real = held[...].reshape(depth, lanes)
    imag = held_turned[...].reshape(depth, lanes)
    for far_or, left in ((0, near), (1, far)):
        out[far_or] = jnp.dot(
            left[:, :depth], real, preferred_element_type=jnp.float32
        ) + jnp.dot(left[:, depth:], imag, preferred_element_type=jnp.float32)


def diagonal_kernel(scale, structure, mine, theirs, panels, panels_far, panels_core, panels_far_core, own, far, diag, left, right, full):
    supernodes, _, rows_half, width = panels.shape
    row_index, col_index = lax.axis_index("prow"), lax.axis_index("pcol")
    rows_dev = 2 * rows_half
    for far_or, (same, cross) in ((0, (panels, panels_core)), (1, (panels_far, panels_far_core))):
        start = (row_index ^ far_or) * rows_dev
        for node in range(supernodes):
            for part in range(2):
                left[node, far_or, part, col_index] = same[node, part]
                left[node, far_or, part, 1 - col_index] = cross[node, part]
            lanes = slice(node * width, (node + 1) * width)
            keep = keep_rows(structure, node, start, rows_dev, width)
            value = -((mine[far_or, :, lanes] + theirs[far_or, :, lanes]) * keep)
            value = value.astype(jnp.bfloat16).astype(jnp.float32)
            column = value.astype(jnp.bfloat16).reshape(2, rows_half, width)
            right[node, far_or, 0] = column
            right[node, far_or, 1] = turned(value).astype(jnp.bfloat16).reshape(2, rows_half, width)
            out = own if far_or == 0 else far
            out[node] = right[node, far_or, 0, col_index]
    depth = 4 * rows_dev
    for node in range(supernodes):
        full[node] = lax.dot_general(
            left[node].reshape(depth, width),
            right[node].reshape(depth, width),
            (((0,), (0,)), ((), ())),
            preferred_element_type=jnp.float32,
        )
    half = width // 2
    diag[...] = full[:, pl.ds(pl.multiple_of(col_index * half, half), half), :] * (1.0 / scale)


def unpack(near, far):
    parity = lax.axis_index("prow") % 2
    low = jnp.where(parity == 0, near, far)
    high = jnp.where(parity == 0, far, near)
    first = lax.broadcasted_iota(jnp.int32, near.shape, 1) < near.shape[1] // 2
    return jnp.where(first, low, swap_halves(high)), jnp.where(first, swap_halves(low), high)


def columns_kernel(own, other, out):
    supernodes, _, rows_half, width = out.shape
    for node in range(supernodes):
        rows = slice(node * rows_half, (node + 1) * rows_half)
        real, imag = unpack(
            own[rows].astype(jnp.float32),
            other[rows].astype(jnp.float32),
        )
        out[node, 0] = real.astype(jnp.bfloat16)
        out[node, 1] = imag.astype(jnp.bfloat16)


def final_kernel(scale, diag_inverse, mine, far, mine_core, far_core, out):
    supernodes, _, width, _ = out.shape
    half = width // 2
    col_index = lax.axis_index("pcol")
    for node in range(supernodes):
        part = slice(node * half, (node + 1) * half)
        for col, near_ref, far_ref in ((col_index, mine, far), (1 - col_index, mine_core, far_core)):
            rows = pl.ds(pl.multiple_of(col * half, half), half)
            real, imag = unpack(near_ref[part] * scale, far_ref[part] * scale)
            out[node, 0, rows] = diag_inverse[node, 0, rows].astype(jnp.float32) - real
            out[node, 1, rows] = diag_inverse[node, 1, rows].astype(jnp.float32) - imag


def solution(mesh):
    rows, cols = mesh.shape["prow"], mesh.shape["pcol"]

    def local(anc_inverse, panels, diag_inverse, structure):
        supernodes, _, rows_half, width = panels.shape
        half = width // 2
        groups = anc_inverse.shape[1]
        rows_dev = anc_inverse.shape[4]
        lanes = supernodes * width
        row_index = lax.axis_index("prow")
        col_index = lax.axis_index("pcol")
        here = row_index // 2
        bf16, f32 = jnp.bfloat16, jnp.float32

        panels = plain(panels)
        panels_far = plain(swap(panels, rows, cols, 1, 1))
        near = anc_inverse.reshape(2 * groups * rows_half, rows_dev).T
        far = swap(near, rows, cols, 1, 1)

        (block,) = call(
            pick_kernel, [((2, rows_half, lanes), bf16)], [structure, panels, panels_far]
        )
        held = jnp.zeros((rows // 2,) + block.shape, bf16)
        held = lax.dynamic_update_index_in_dim(held, block, here, 0)
        arrived = [swap(block, rows, cols, mask0, mask1) for mask0, mask1 in MASKS]
        panels_core = swap_core(panels)
        panels_far_core = swap_core(panels_far)
        for (mask0, mask1), value in zip(MASKS, arrived):
            step = jnp.where(col_index == 0, mask0, mask1) // 2
            held = lax.dynamic_update_index_in_dim(held, value, here ^ step, 0)
        size = 8
        while size < rows:
            count = size // 2
            start = (here // count) * count
            own = lax.dynamic_slice_in_dim(held, start, count, 0)
            other = swap(own, rows, cols, size, size)
            held = lax.dynamic_update_slice_in_dim(held, other, start ^ count, 0)
            size *= 2

        held = after(held, panels_core, panels_far_core)
        (partial,) = call(
            functools.partial(product_kernel, width),
            [((2, rows_dev, lanes), f32)],
            [near, far, held],
            [pltpu.VMEM(held.shape, bf16)],
        )
        scale = 2 ** max(0, math.ceil(math.log2(groups * 2 * rows_half / 24)))
        pieces = (supernodes, 2, 2, cols, rows_half, width)
        own, send, diag = call(
            functools.partial(diagonal_kernel, float(scale)),
            [((supernodes, rows_half, width), bf16)] * 2 + [((supernodes, half, width), f32)],
            [structure, partial, swap_core(partial), panels, panels_far, panels_core, panels_far_core],
            [pltpu.VMEM(pieces, bf16), pltpu.VMEM(pieces, bf16), pltpu.VMEM((supernodes, width, width), f32)],
        )
        f16 = jnp.float16
        count = supernodes * half
        columns_rows = supernodes * rows_half
        term = diag.reshape(count, width).astype(f16)
        terms = [term] + [swap(term, rows, cols, mask0, mask1) for mask0, mask1 in MASKS_SUM]
        first, second, third, fourth = [t.astype(f32) for t in terms]
        term = (first + second) + (third + fourth)
        size = 8
        while size < rows:
            term = term + swap(term, rows, cols, size, size)
            size *= 2
        mine = term.astype(f16)
        other = swap(
            jnp.concatenate([mine, send.reshape(columns_rows, width).astype(f16)]), rows, cols, 1, 1
        )
        far = other[:count]
        (columns,) = call(
            columns_kernel,
            [((supernodes, 2, rows_half, width), bf16)],
            [own.reshape(columns_rows, width), other[count:].astype(f32)],
        )
        pieces = [v.astype(f32) for v in (mine, far, swap_core(mine), swap_core(far))]
        (diag,) = call(
            functools.partial(final_kernel, float(scale)),
            [((supernodes, 2, width, width), f32)],
            [diag_inverse] + pieces,
        )
        return columns, diag

    in_specs = (
        P("pole", None, "pcol", None, "prow"),
        P("pole", None, ("prow", "pcol"), None),
        P("pole", None, None, None),
        P(),
    )
    out_specs = (P("pole", None, ("prow", "pcol"), None), P("pole", None, None, None))
    return jax.shard_map(local, mesh=mesh, in_specs=in_specs, out_specs=out_specs, check_vma=False)
```

```python
import functools
import math

import jax
import jax.numpy as jnp
from jax import lax
from jax.experimental import pallas as pl
from jax.experimental.layout import Layout, with_layout_constraint
from jax.experimental.pallas import tpu as pltpu
from jax.sharding import PartitionSpec as P

AXES = ("prow", "pcol")
MASKS = (2, 4, 6)
MASKS_SUM = (6, 4, 2)
VMEM = pl.BlockSpec(memory_space=pltpu.VMEM)
HBM = pl.BlockSpec(memory_space=pltpu.HBM)


def swap(value, rows, cols, mask0, mask1):
    pairs = []
    for row in range(rows):
        for col in range(cols):
            mask = mask0 if col == 0 else mask1
            pairs.append((row * cols + col, (row ^ mask) * cols + col))
    return lax.ppermute(value, AXES, pairs)


def swap_core(value):
    return lax.ppermute(value, "pcol", [(0, 1), (1, 0)])


def after(value, *others):
    return lax.optimization_barrier((value,) + others)[0]


def plain(value):
    return with_layout_constraint(value, Layout(tuple(range(value.ndim))))


def call(kernel, outs, operands, scratch=(), cost=0, space=VMEM, limit=0):
    shapes = [jax.ShapeDtypeStruct(shape, dtype) for shape, dtype in outs]
    size = sum(v.size * v.dtype.itemsize for v in list(operands) + shapes)
    return pl.pallas_call(
        kernel,
        out_shape=shapes,
        in_specs=[space] * len(operands),
        out_specs=[VMEM] * len(shapes),
        scratch_shapes=list(scratch),
        cost_estimate=pl.CostEstimate(flops=0, bytes_accessed=cost or size, transcendentals=0),
        compiler_params=pltpu.CompilerParams(vmem_limit_bytes=limit or 2 * size + (4 << 20)),
    )(*operands)


def keep_rows(structure, node, start, count, width):
    blocks = structure.shape[1]
    row = start + lax.broadcasted_iota(jnp.int32, (count, blocks), 0)
    hit = row // width == lax.broadcasted_iota(jnp.int32, (count, blocks), 1)
    table = structure[node : node + 1, :].astype(jnp.float32)
    return jnp.sum(jnp.where(hit, table, 0.0), axis=1, keepdims=True)


def swap_halves(value):
    half = value.shape[-1] // 2
    return jnp.concatenate([value[:, half:], value[:, :half]], axis=-1)


def turned(value):
    lane = lax.broadcasted_iota(jnp.int32, value.shape, 1)
    other = swap_halves(value)
    return jnp.where(lane < value.shape[-1] // 2, -other, other)


def packed(source, node, low, parity):
    real = source[node, 0].astype(jnp.float32)
    imag = source[node, 1].astype(jnp.float32)
    left = jnp.where(low, real, swap_halves(imag))
    right = jnp.where(low, swap_halves(real), imag)
    return jnp.where(parity == 0, left, right)


def first_kernel(
    matrix_in, panels_in, diag_in, structure_in, across, panels, diag_inverse, keep, keep_far, own, matrix, structure, done
):
    pairs = ((panels_in, panels), (structure_in, structure), (matrix_in, matrix), (diag_in, diag_inverse))
    copies = [pltpu.make_async_copy(*pair, done.at[index]) for index, pair in enumerate(pairs)]
    for copy in copies:
        copy.start()
    for copy in copies:
        copy.wait()
    supernodes, _, rows_half, width = panels.shape
    groups, rows_dev = matrix.shape[1], matrix.shape[4]
    row_index, col_index = lax.axis_index("prow"), lax.axis_index("pcol")
    for part in range(2):
        across[part] = matrix[part].reshape(groups * rows_half, rows_dev).T
    low = lax.broadcasted_iota(jnp.int32, (rows_half, width), 1) < width // 2
    for node in range(supernodes):
        lanes = slice(node * width, (node + 1) * width)
        for far_or in range(2):
            start = (row_index ^ far_or) * rows_dev
            value = keep_rows(structure, node, start, rows_dev, width)
            keep[far_or, :, node : node + 1] = value
            part = keep_rows(structure, node, start + col_index * rows_half, rows_half, width)
            if far_or == 0:
                own[:, lanes] = (packed(panels, node, low, row_index % 2) * part).astype(jnp.bfloat16)
            else:
                keep_far[:, node : node + 1] = part


def pick_kernel(own, keep_far, panels_far, block):
    supernodes, _, rows_half, width = panels_far.shape
    parity = lax.axis_index("prow") % 2
    low = lax.broadcasted_iota(jnp.int32, (rows_half, width), 1) < width // 2
    block[parity] = own[...]
    for node in range(supernodes):
        lanes = slice(node * width, (node + 1) * width)
        value = packed(panels_far, node, low, parity) * keep_far[:, node : node + 1]
        block[1 - parity, :, lanes] = value.astype(jnp.bfloat16)


def merge_kernel(block, block_core, near, near_core, chip, first, second):
    carry = lax.axis_index("pcol") == 0
    _, rows_half, _ = block.shape
    for core, source in ((0, block_core), (1, block)):
        for x in range(2):
            rows = slice(x * rows_half, (x + 1) * rows_half)
            chip[core, rows] = source[x]
            first[core, rows] = jnp.where(carry, near[core, rows], source[x])
            second[core, rows] = jnp.where(carry, near_core[core, rows], source[x])


def product_kernel(width, near, near_core, far_0, far_1, held, out):
    count, _, rows_dev, lanes = held.shape
    depth = count * rows_dev
    rights = [held[:, core].reshape(depth, lanes) for core in range(2)]
    for far_or, lefts in ((0, (near_core, near)), (1, (far_0, far_1))):
        real, imag = [
            sum(
                jnp.dot(left[part], right, preferred_element_type=jnp.float32)
                for left, right in zip(lefts, rights)
            )
            for part in range(2)
        ]
        for node in range(lanes // width):
            part = slice(node * width, (node + 1) * width)
            out[far_or, :, part] = real[:, part] + turned(imag[:, part])


def left_kernel(panels, panels_far, panels_core, panels_far_core, out, rows):
    supernodes, _, rows_half, width = panels.shape
    for node in range(supernodes):
        for part in range(2):
            for far_or, (same, cross) in ((0, (panels, panels_core)), (1, (panels_far, panels_far_core))):
                rows[far_or, 0] = cross[node, part]
                rows[far_or, 1] = same[node, part]
            out[node, part] = rows[...].reshape(4 * rows_half, width).T


def diagonal_kernel(scale, kept, product, left, own, send, diag, columns):
    supernodes, _, width, _ = left.shape
    rows_dev = product.shape[1]
    rows_half = rows_dev // 2
    for node in range(supernodes):
        lanes = slice(node * width, (node + 1) * width)
        for far_or in range(2):
            keep = kept[far_or, :, node : node + 1]
            value = (-(product[far_or, :, lanes] * keep)).astype(jnp.bfloat16)
            columns[far_or] = value
            low, high = value[:rows_half], value[rows_half:]
            if far_or == 0:
                send[0, node], own[node] = low, high
            else:
                send[1, node], send[2, node] = low, high
        right = columns[...].reshape(2 * rows_dev, width)
        real = jnp.dot(left[node, 0], right, preferred_element_type=jnp.float32)
        imag = jnp.dot(left[node, 1], right, preferred_element_type=jnp.float32)
        diag[node] = (real + turned(imag)) * (1.0 / scale)


def unpack(near, far):
    parity = lax.axis_index("prow") % 2
    low = jnp.where(parity == 0, near, far)
    high = jnp.where(parity == 0, far, near)
    first = lax.broadcasted_iota(jnp.int32, near.shape, 1) < near.shape[1] // 2
    return jnp.where(first, low, swap_halves(high)), jnp.where(first, swap_halves(low), high)


def columns_kernel(own, own_core, other, other_core, out):
    supernodes, _, rows_half, width = out.shape
    first = lax.axis_index("pcol") == 0
    for node in range(supernodes):
        rows = slice(node * rows_half, (node + 1) * rows_half)
        near = jnp.where(first, own_core[rows].astype(jnp.float32), own[rows].astype(jnp.float32))
        far = jnp.where(first, other[rows], other_core[rows])
        real, imag = unpack(near, far)
        out[node, 0] = real.astype(jnp.bfloat16)
        out[node, 1] = imag.astype(jnp.bfloat16)


def final_kernel(scale, diag_inverse, mine, far, mine_core, far_core, out):
    supernodes, _, width, _ = out.shape
    first = lax.axis_index("pcol") == 0
    for node in range(supernodes):
        rows = slice(node * width, (node + 1) * width)
        near_value = jnp.where(first, mine_core[rows], mine[rows]) * scale
        far_value = jnp.where(first, far_core[rows], far[rows]) * scale
        real, imag = unpack(near_value, far_value)
        out[node, 0] = diag_inverse[node, 0].astype(jnp.float32) - real
        out[node, 1] = diag_inverse[node, 1].astype(jnp.float32) - imag


def solution(mesh):
    rows, cols = mesh.shape["prow"], mesh.shape["pcol"]

    def local(anc_inverse, panels, diag_inverse, structure):
        supernodes, _, rows_half, width = panels.shape
        half = width // 2
        groups = anc_inverse.shape[1]
        rows_dev = anc_inverse.shape[4]
        lanes = supernodes * width
        row_index = lax.axis_index("prow")
        col_index = lax.axis_index("pcol")
        here = row_index // 2
        bf16, f32 = jnp.bfloat16, jnp.float32

        panels = plain(panels)
        panels_far = plain(swap(panels, rows, cols, 1, 1))
        chip_shape = (2, rows_dev, lanes)
        shape = (2, rows_dev, groups * rows_half)
        near, panels, diag_inverse, keep, keep_far, own = call(
            first_kernel,
            [
                (shape, bf16),
                (panels.shape, bf16),
                (diag_inverse.shape, bf16),
                ((2, rows_dev, 128), f32),
                ((rows_half, 128), f32),
                ((rows_half, lanes), bf16),
            ],
            [pltpu.with_memory_space_constraint(v, pltpu.HBM) for v in (anc_inverse, panels, diag_inverse, structure)],
            [
                pltpu.VMEM(anc_inverse.shape, bf16),
                pltpu.VMEM(structure.shape, jnp.int32),
                pltpu.SemaphoreType.DMA((4,)),
            ],
            cost=12 << 20,
            space=HBM,
        )
        near_core = swap_core(near)
        panels_core = swap_core(panels)
        (block,) = call(pick_kernel, [((2, rows_half, lanes), bf16)], [own, keep_far, panels_far])
        if shape == chip_shape:
            chip, first, second = call(
                merge_kernel, [(chip_shape, bf16)] * 3, [block, swap_core(block), near, near_core]
            )
            far_0 = far_1 = None
        else:
            chip = first = second = jnp.stack([swap_core(block), block]).reshape(chip_shape)
            far_1 = swap(near, rows, cols, 1, 1)
            far_0 = swap_core(far_1)
        held = jnp.zeros((rows // 2,) + chip_shape, bf16)
        held = lax.dynamic_update_index_in_dim(held, chip, here, 0)
        arrived = [swap(value, rows, cols, 1, mask) for value, mask in zip((first, second, chip), MASKS)]
        if far_0 is None:
            far_0, far_1 = swap_core(arrived[0]), swap_core(arrived[1])
        panels_far_core = swap_core(panels_far)
        (left,) = call(
            left_kernel,
            [((supernodes, 2, width, 2 * rows_dev), bf16)],
            [panels, panels_far, panels_core, panels_far_core],
            [pltpu.VMEM((2, cols, rows_half, width), bf16)],
            cost=6 << 20,
        )
        for index, (mask, value) in enumerate(zip(MASKS, arrived)):
            held = lax.dynamic_update_index_in_dim(held, value, here ^ (mask // 2), 0)
            held = after(held, left) if index == 0 else held
        size = 8
        while size < rows:
            count = size // 2
            start = (here // count) * count
            own = lax.dynamic_slice_in_dim(held, start, count, 0)
            other = swap(own, rows, cols, 1, size)
            held = lax.dynamic_update_slice_in_dim(held, other, start ^ count, 0)
            size *= 2

        (product,) = call(
            functools.partial(product_kernel, width),
            [((2, rows_dev, lanes), f32)],
            [near, near_core, far_0, far_1, held],
        )
        scale = 2 ** max(0, math.ceil(math.log2(groups * 2 * rows_half / 24)))
        own, send, diag = call(
            functools.partial(diagonal_kernel, float(scale)),
            [
                ((supernodes, rows_half, width), bf16),
                ((3, supernodes, rows_half, width), bf16),
                ((supernodes, width, width), f32),
            ],
            [keep, product, left],
            [pltpu.VMEM((2, rows_dev, width), bf16)],
        )
        f16 = jnp.float16
        count = supernodes * width
        some = supernodes * rows_half
        term = diag.reshape(count, width).astype(f16)
        sent = swap_core(send.reshape(3 * some, width))
        last = jnp.concatenate([sent[some:].astype(f16), term[2 * some :]])
        last = jnp.where(col_index == 0, last, term)
        terms = [swap(v, rows, cols, 1, mask) for mask, v in zip(MASKS_SUM, (term, term, last))]
        other = terms[2]
        first, second, third = [t.astype(f32) for t in terms]
        total = (term.astype(f32) + first) + (second + third)
        size = 8
        while size < rows:
            total = total + swap(total, rows, cols, 1, size)
            size *= 2
        mine = total.astype(f16)
        far = swap(mine, rows, cols, 2, 1)
        (columns,) = call(
            columns_kernel,
            [((supernodes, 2, rows_half, width), bf16)],
            [own.reshape(some, width), sent[:some], other[:some].astype(f32), swap_core(other[some : 2 * some]).astype(f32)],
            cost=4 << 20,
        )
        far_sent = far
        far_sent = after(far, columns)
        pieces = [v.astype(f32) for v in (mine, far, swap_core(mine), swap_core(far_sent))]
        (diag,) = call(
            functools.partial(final_kernel, float(scale)),
            [((supernodes, 2, width, width), f32)],
            [diag_inverse] + pieces,
        )
        return columns, diag

    in_specs = (
        P("pole", None, "pcol", None, "prow"),
        P("pole", None, ("prow", "pcol"), None),
        P("pole", None, None, None),
        P(),
    )
    out_specs = (P("pole", None, ("prow", "pcol"), None), P("pole", None, None, None))
    return jax.shard_map(local, mesh=mesh, in_specs=in_specs, out_specs=out_specs, check_vma=False)
```

```python
import functools
import math

import jax
import jax.numpy as jnp
from jax import lax
from jax.experimental import pallas as pl
from jax.experimental.layout import Layout, with_layout_constraint
from jax.experimental.pallas import tpu as pltpu
from jax.sharding import PartitionSpec as P

AXES = ("prow", "pcol")
MASKS = (4, 2, 6)
MASKS_SUM = (4, 2, 6)
VMEM = pl.BlockSpec(memory_space=pltpu.VMEM)
HBM = pl.BlockSpec(memory_space=pltpu.HBM)


def steps_of(count):
    steps = [0] + [mask // 2 for mask in MASKS]
    while len(steps) < count:
        steps = steps + [step ^ len(steps) for step in steps]
    return steps


def swap(value, rows, cols, mask0, mask1):
    pairs = []
    for row in range(rows):
        for col in range(cols):
            mask = mask0 if col == 0 else mask1
            pairs.append((row * cols + col, (row ^ mask) * cols + col))
    return lax.ppermute(value, AXES, pairs)


def swap_core(value):
    return lax.ppermute(value, "pcol", [(0, 1), (1, 0)])


def after(value, *others):
    return lax.optimization_barrier((value,) + others)[0]


def plain(value):
    return with_layout_constraint(value, Layout(tuple(range(value.ndim))))


def call(kernel, outs, operands, scratch=(), cost=0, space=VMEM, out_space=VMEM, limit=0):
    shapes = [jax.ShapeDtypeStruct(shape, dtype) for shape, dtype in outs]
    size = sum(v.size * v.dtype.itemsize for v in list(operands) + shapes)
    return pl.pallas_call(
        kernel,
        out_shape=shapes,
        in_specs=[space] * len(operands),
        out_specs=[out_space] * len(shapes),
        scratch_shapes=list(scratch),
        cost_estimate=pl.CostEstimate(flops=0, bytes_accessed=cost or size, transcendentals=0),
        compiler_params=pltpu.CompilerParams(vmem_limit_bytes=limit or 2 * size + (4 << 20)),
    )(*operands)


def keep_rows(structure, node, start, count, width):
    blocks = structure.shape[1]
    row = start + lax.broadcasted_iota(jnp.int32, (count, blocks), 0)
    hit = row // width == lax.broadcasted_iota(jnp.int32, (count, blocks), 1)
    table = structure[node : node + 1, :].astype(jnp.float32)
    return jnp.sum(jnp.where(hit, table, 0.0), axis=1, keepdims=True)


def swap_halves(value):
    half = value.shape[-1] // 2
    return jnp.concatenate([value[:, half:], value[:, :half]], axis=-1)


def turned(value):
    lane = lax.broadcasted_iota(jnp.int32, value.shape, 1)
    other = swap_halves(value)
    return jnp.where(lane < value.shape[-1] // 2, -other, other)


def packed(source, node, low, parity):
    real = source[node, 0].astype(jnp.float32)
    imag = source[node, 1].astype(jnp.float32)
    left = jnp.where(low, real, swap_halves(imag))
    right = jnp.where(low, swap_halves(real), imag)
    return jnp.where(parity == 0, left, right)


def first_kernel(
    matrix_in, panels_in, diag_in, structure_in, across, panels, diag_inverse, keep, keep_far, own, matrix, structure, done
):
    pairs = ((panels_in, panels), (structure_in, structure), (matrix_in, matrix), (diag_in, diag_inverse))
    copies = [pltpu.make_async_copy(*pair, done.at[index]) for index, pair in enumerate(pairs)]
    for copy in copies:
        copy.start()
    for copy in copies:
        copy.wait()
    supernodes, _, rows_half, width = panels.shape
    groups, rows_dev = matrix.shape[1], matrix.shape[4]
    row_index, col_index = lax.axis_index("prow"), lax.axis_index("pcol")
    here = row_index // 2
    for part in range(2):
        pieces = [matrix[part, pl.ds(2 * (here ^ step), 2)] for step in steps_of(groups // 2)]
        across[part] = jnp.concatenate(pieces).reshape(groups * rows_half, rows_dev).T
    low = lax.broadcasted_iota(jnp.int32, (rows_half, width), 1) < width // 2
    for node in range(supernodes):
        lanes = slice(node * width, (node + 1) * width)
        for far_or in range(2):
            start = (row_index ^ far_or) * rows_dev
            value = keep_rows(structure, node, start, rows_dev, width)
            keep[far_or, :, node : node + 1] = value
            part = keep_rows(structure, node, start + col_index * rows_half, rows_half, width)
            if far_or == 0:
                own[:, lanes] = (packed(panels, node, low, row_index % 2) * part).astype(jnp.bfloat16)
            else:
                keep_far[:, node : node + 1] = part


def pick_kernel(own, keep_far, panels_far, block):
    supernodes, _, rows_half, width = panels_far.shape
    parity = lax.axis_index("prow") % 2
    low = lax.broadcasted_iota(jnp.int32, (rows_half, width), 1) < width // 2
    block[parity] = own[...]
    for node in range(supernodes):
        lanes = slice(node * width, (node + 1) * width)
        value = packed(panels_far, node, low, parity) * keep_far[:, node : node + 1]
        block[1 - parity, :, lanes] = value.astype(jnp.bfloat16)


def merge_kernel(block, block_core, near, near_core, chip, first, second):
    carry = lax.axis_index("pcol") == 0
    _, rows_half, _ = block.shape
    for core, source in ((0, block_core), (1, block)):
        for x in range(2):
            rows = slice(x * rows_half, (x + 1) * rows_half)
            chip[core, rows] = source[x]
            first[core, rows] = jnp.where(carry, near[core, rows], source[x])
            second[core, rows] = jnp.where(carry, near_core[core, rows], source[x])


def product_kernel(near, near_core, far_0, far_1, held, out):
    count, _, rows_dev, lanes = held.shape
    depth = count * rows_dev
    for core, lefts in ((0, (near_core, far_0)), (1, (near, far_1))):
        right = held[:, core].reshape(depth, lanes)
        for far_or, left in enumerate(lefts):
            value = jnp.dot(left[...].reshape(2 * rows_dev, depth), right, preferred_element_type=jnp.float32)
            value = value.reshape(out.shape[1:])
            out[far_or] = value if core == 0 else out[far_or] + value


def whole_kernel(scale, near, near_core, far_0, far_1, block_0, block_1, block_2, block_3, kept, left, own, send, diag, columns):
    supernodes, rows_half, width = own.shape
    _, rows_dev, depth = near.shape
    blocks = (block_0, block_1, block_2, block_3)
    right = jnp.concatenate([block[core] for core in range(2) for block in blocks])
    for far_or, pair in enumerate(((near_core, near), (far_0, far_1))):
        both = jnp.concatenate([part[...].reshape(2 * rows_dev, depth) for part in pair], axis=1)
        value = jnp.dot(both, right, preferred_element_type=jnp.float32)
        for node in range(supernodes):
            lanes = slice(node * width, (node + 1) * width)
            keep = kept[far_or, :, node : node + 1]
            column = value[:rows_dev, lanes] + turned(value[rows_dev:, lanes])
            column = (-(column * keep)).astype(jnp.bfloat16)
            columns[node, far_or] = column
            low, high = column[:rows_half], column[rows_half:]
            if far_or == 0:
                send[0, node], own[node] = low, high
            else:
                send[1, node], send[2, node] = low, high
    for node in range(supernodes):
        both = jnp.dot(
            left[node].reshape(2 * width, 2 * rows_dev),
            columns[node].reshape(2 * rows_dev, width),
            preferred_element_type=jnp.float32,
        )
        diag[node] = (both[:width] + turned(both[width:])) * (1.0 / scale)


def left_kernel(panels, panels_far, panels_core, panels_far_core, out, rows):
    supernodes, _, rows_half, width = panels.shape
    for node in range(supernodes):
        for part in range(2):
            for far_or, (same, cross) in ((0, (panels, panels_core)), (1, (panels_far, panels_far_core))):
                rows[far_or, 0] = cross[node, part]
                rows[far_or, 1] = same[node, part]
            out[node, part] = rows[...].reshape(4 * rows_half, width).T


def diagonal_kernel(scale, kept, product, left, own, send, diag, columns):
    supernodes, _, width, _ = left.shape
    rows_dev = product.shape[2]
    rows_half = rows_dev // 2
    for node in range(supernodes):
        lanes = slice(node * width, (node + 1) * width)
        for far_or in range(2):
            keep = kept[far_or, :, node : node + 1]
            value = product[far_or, 0, :, lanes] + turned(product[far_or, 1, :, lanes])
            value = (-(value * keep)).astype(jnp.bfloat16)
            columns[far_or] = value
            low, high = value[:rows_half], value[rows_half:]
            if far_or == 0:
                send[0, node], own[node] = low, high
            else:
                send[1, node], send[2, node] = low, high
        right = columns[...].reshape(2 * rows_dev, width)
        both = jnp.dot(left[node].reshape(2 * width, 2 * rows_dev), right, preferred_element_type=jnp.float32)
        diag[node] = (both[:width] + turned(both[width:])) * (1.0 / scale)


def unpack(near, far):
    parity = lax.axis_index("prow") % 2
    low = jnp.where(parity == 0, near, far)
    high = jnp.where(parity == 0, far, near)
    first = lax.broadcasted_iota(jnp.int32, near.shape, 1) < near.shape[1] // 2
    return jnp.where(first, low, swap_halves(high)), jnp.where(first, swap_halves(low), high)


def columns_kernel(own, own_core, other, other_core, out):
    supernodes, _, rows_half, width = out.shape
    first = lax.axis_index("pcol") == 0
    for node in range(supernodes):
        rows = slice(node * rows_half, (node + 1) * rows_half)
        near = jnp.where(first, own_core[rows].astype(jnp.float32), own[rows].astype(jnp.float32))
        far = jnp.where(first, other[rows], other_core[rows])
        real, imag = unpack(near, far)
        out[node, 0] = real.astype(jnp.bfloat16)
        out[node, 1] = imag.astype(jnp.bfloat16)


def final_kernel(scale, diag_inverse, mine, far, mine_core, far_core, out, value, done):
    supernodes, _, width, _ = out.shape
    first = lax.axis_index("pcol") == 0
    copies = [pltpu.make_async_copy(value.at[node], out.at[node], done.at[node]) for node in range(supernodes)]
    for node in range(supernodes):
        rows = slice(node * width, (node + 1) * width)
        near_value = jnp.where(first, mine_core[rows], mine[rows]) * scale
        far_value = jnp.where(first, far_core[rows], far[rows]) * scale
        real, imag = unpack(near_value, far_value)
        value[node, 0] = diag_inverse[node, 0].astype(jnp.float32) - real
        value[node, 1] = diag_inverse[node, 1].astype(jnp.float32) - imag
        copies[node].start()
    for copy in copies:
        copy.wait()


def solution(mesh):
    rows, cols = mesh.shape["prow"], mesh.shape["pcol"]

    def local(anc_inverse, panels, diag_inverse, structure):
        supernodes, _, rows_half, width = panels.shape
        half = width // 2
        groups = anc_inverse.shape[1]
        rows_dev = anc_inverse.shape[4]
        lanes = supernodes * width
        row_index = lax.axis_index("prow")
        col_index = lax.axis_index("pcol")
        here = row_index // 2
        bf16, f32 = jnp.bfloat16, jnp.float32

        panels = plain(panels)
        panels_far = plain(swap(panels, rows, cols, 1, 1))
        chip_shape = (2, rows_dev, lanes)
        shape = (2, rows_dev, groups * rows_half)
        near, panels, diag_inverse, keep, keep_far, own = call(
            first_kernel,
            [
                (shape, bf16),
                (panels.shape, bf16),
                (diag_inverse.shape, bf16),
                ((2, rows_dev, 128), f32),
                ((rows_half, 128), f32),
                ((rows_half, lanes), bf16),
            ],
            [pltpu.with_memory_space_constraint(v, pltpu.HBM) for v in (anc_inverse, panels, diag_inverse, structure)],
            [
                pltpu.VMEM(anc_inverse.shape, bf16),
                pltpu.VMEM(structure.shape, jnp.int32),
                pltpu.SemaphoreType.DMA((4,)),
            ],
            cost=12 << 20,
            space=HBM,
        )
        near_core = swap_core(near)
        panels_core = swap_core(panels)
        (block,) = call(pick_kernel, [((2, rows_half, lanes), bf16)], [own, keep_far, panels_far])
        if shape == chip_shape:
            chip, first, second = call(
                merge_kernel, [(chip_shape, bf16)] * 3, [block, swap_core(block), near, near_core]
            )
            far_0 = far_1 = None
        else:
            chip = first = second = jnp.stack([swap_core(block), block]).reshape(chip_shape)
            far_1 = swap(near, rows, cols, 1, 1)
            far_0 = swap_core(far_1)
        arrived = [swap(value, rows, cols, 1, mask) for value, mask in zip((first, second, chip), MASKS)]
        if far_0 is None:
            far_0, far_1 = swap_core(arrived[0]), swap_core(arrived[1])
        panels_far_core = swap_core(panels_far)
        (left,) = call(
            left_kernel,
            [((supernodes, 2, width, 2 * rows_dev), bf16)],
            [panels, panels_far, panels_core, panels_far_core],
            [pltpu.VMEM((2, cols, rows_half, width), bf16)],
        )
        scale = 2 ** max(0, math.ceil(math.log2(groups * 2 * rows_half / 24)))
        outs = [
            ((supernodes, rows_half, width), bf16),
            ((3, supernodes, rows_half, width), bf16),
            ((supernodes, width, width), f32),
        ]
        sums = (2, 2, rows_dev, lanes)
        columns_scratch = pltpu.VMEM((2, rows_dev, width), bf16)
        lefts = [near, near_core, far_0, far_1]
        arrived = list(lax.optimization_barrier(tuple(arrived)))
        if rows == 8:
            own, send, diag = call(
                functools.partial(whole_kernel, float(scale)),
                outs,
                lefts + [chip] + arrived + [keep, left],
                [pltpu.VMEM((supernodes, 2, rows_dev, width), bf16)],
            )
        else:
            held = jnp.stack([chip] + arrived)
            size = 8
            while size < rows:
                held = jnp.concatenate([held, swap(held, rows, cols, 1, size)])
                size *= 2
            (product,) = call(product_kernel, [(sums, f32)], lefts + [held])
            own, send, diag = call(
                functools.partial(diagonal_kernel, float(scale)), outs, [keep, product, left], [columns_scratch]
            )
        f16 = jnp.float16
        count = supernodes * width
        some = supernodes * rows_half
        term = diag.reshape(count, width).astype(f16)
        sent = swap_core(send.reshape(3 * some, width))
        last = jnp.concatenate([sent[some:].astype(f16), term[2 * some :]])
        last = jnp.where(col_index == 0, last, term)
        terms = [swap(v, rows, cols, 1, mask) for mask, v in zip(MASKS_SUM, (term, term, last))]
        other = terms[2]
        first, second, third = [t.astype(f32) for t in terms]
        total = (term.astype(f32) + first) + (second + third)
        size = 8
        while size < rows:
            total = total + swap(total, rows, cols, 1, size)
            size *= 2
        mine = total.astype(f16)
        far = swap(mine, rows, cols, 2, 1)
        (columns,) = call(
            columns_kernel,
            [((supernodes, 2, rows_half, width), bf16)],
            [own.reshape(some, width), sent[:some], other[:some].astype(f32), swap_core(other[some : 2 * some]).astype(f32)],
            cost=4 << 20,
        )
        far_sent = far
        far_sent = after(far, columns)
        pieces = [v.astype(f32) for v in (mine, far, swap_core(mine), swap_core(far_sent))]
        (diag,) = call(
            functools.partial(final_kernel, float(scale)),
            [((supernodes, 2, width, width), f32)],
            [diag_inverse] + pieces,
            [pltpu.VMEM((supernodes, 2, width, width), f32), pltpu.SemaphoreType.DMA((supernodes,))],
            out_space=HBM,
        )
        return columns, diag

    in_specs = (
        P("pole", None, "pcol", None, "prow"),
        P("pole", None, ("prow", "pcol"), None),
        P("pole", None, None, None),
        P(),
    )
    out_specs = (P("pole", None, ("prow", "pcol"), None), P("pole", None, None, None))
    return jax.shard_map(local, mesh=mesh, in_specs=in_specs, out_specs=out_specs, check_vma=False)
```

```python
import functools
import math

import jax
import jax.numpy as jnp
from jax import lax
from jax.experimental import pallas as pl
from jax.experimental.layout import Layout, with_layout_constraint
from jax.experimental.pallas import tpu as pltpu
from jax.sharding import PartitionSpec as P

AXES = ("prow", "pcol")
MASKS = (4, 2, 6)
MASKS_SUM = (2, 4, 6)
STEP, LEVELS, LEVEL_ROWS = 16, 5, 16
VMEM = pl.BlockSpec(memory_space=pltpu.VMEM)
HBM = pl.BlockSpec(memory_space=pltpu.HBM)


def steps_of(count):
    steps = [0] + [mask // 2 for mask in MASKS]
    while len(steps) < count:
        steps = steps + [step ^ len(steps) for step in steps]
    return steps


def swap(value, rows, cols, mask0, mask1):
    pairs = []
    for row in range(rows):
        for col in range(cols):
            mask = mask0 if col == 0 else mask1
            pairs.append((row * cols + col, (row ^ mask) * cols + col))
    return lax.ppermute(value, AXES, pairs)


def power(level, first, step):
    value = jnp.full(level.shape, 2.0**first, jnp.float32)
    for count in range(1, LEVELS + 1):
        value = jnp.where(level > count - 0.5, 2.0 ** (first + step * count), value)
    return value


def level_of(peak, head):
    level = jnp.zeros(peak.shape, jnp.float32)
    for count in range(1, LEVELS + 1):
        level += jnp.where(peak < 2.0 ** (head - STEP * count), 1.0, 0.0)
    return level


def largest(value):
    return jnp.max(jnp.max(jnp.abs(value), axis=0, keepdims=True), axis=1, keepdims=True)


def swap_core(value):
    return lax.ppermute(value, "pcol", [(0, 1), (1, 0)])


def after(value, *others):
    return lax.optimization_barrier((value,) + others)[0]


def plain(value):
    return with_layout_constraint(value, Layout(tuple(range(value.ndim))))


def call(kernel, outs, operands, scratch=(), cost=0, space=VMEM, out_space=VMEM, limit=0):
    shapes = [jax.ShapeDtypeStruct(shape, dtype) for shape, dtype in outs]
    size = sum(v.size * v.dtype.itemsize for v in list(operands) + shapes)
    return pl.pallas_call(
        kernel,
        out_shape=shapes,
        in_specs=[space] * len(operands),
        out_specs=[out_space] * len(shapes),
        scratch_shapes=list(scratch),
        cost_estimate=pl.CostEstimate(flops=0, bytes_accessed=cost or size, transcendentals=0),
        compiler_params=pltpu.CompilerParams(vmem_limit_bytes=limit or 2 * size + (4 << 20)),
    )(*operands)


def keep_rows(structure, node, start, count, width):
    blocks = structure.shape[1]
    row = start + lax.broadcasted_iota(jnp.int32, (count, blocks), 0)
    hit = row // width == lax.broadcasted_iota(jnp.int32, (count, blocks), 1)
    table = structure[node : node + 1, :].astype(jnp.float32)
    return jnp.sum(jnp.where(hit, table, 0.0), axis=1, keepdims=True)


def swap_halves(value):
    half = value.shape[-1] // 2
    return jnp.concatenate([value[:, half:], value[:, :half]], axis=-1)


def turned(value):
    lane = lax.broadcasted_iota(jnp.int32, value.shape, 1)
    other = swap_halves(value)
    return jnp.where(lane < value.shape[-1] // 2, -other, other)


def packed(source, node, low, parity):
    real = source[node, 0].astype(jnp.float32)
    imag = source[node, 1].astype(jnp.float32)
    left = jnp.where(low, real, swap_halves(imag))
    right = jnp.where(low, swap_halves(real), imag)
    return jnp.where(parity == 0, left, right)


def first_kernel(
    matrix_in, panels_in, diag_in, structure_in, across, panels, diag_inverse, keep, keep_far, own, matrix, structure, done
):
    pairs = ((panels_in, panels), (structure_in, structure), (matrix_in, matrix), (diag_in, diag_inverse))
    copies = [pltpu.make_async_copy(*pair, done.at[index]) for index, pair in enumerate(pairs)]
    for copy in copies:
        copy.start()
    for copy in copies:
        copy.wait()
    supernodes, _, rows_half, width = panels.shape
    groups, rows_dev = matrix.shape[1], matrix.shape[4]
    row_index, col_index = lax.axis_index("prow"), lax.axis_index("pcol")
    here = row_index // 2
    for part in range(2):
        pieces = [matrix[part, pl.ds(2 * (here ^ step), 2)] for step in steps_of(groups // 2)]
        across[part] = jnp.concatenate(pieces).reshape(groups * rows_half, rows_dev).T
    low = lax.broadcasted_iota(jnp.int32, (rows_half, width), 1) < width // 2
    for node in range(supernodes):
        lanes = slice(node * width, (node + 1) * width)
        for far_or in range(2):
            start = (row_index ^ far_or) * rows_dev
            value = keep_rows(structure, node, start, rows_dev, width)
            keep[far_or, :, node : node + 1] = value
            part = keep_rows(structure, node, start + col_index * rows_half, rows_half, width)
            if far_or == 0:
                own[:, lanes] = (packed(panels, node, low, row_index % 2) * part).astype(jnp.bfloat16)
            else:
                keep_far[:, node : node + 1] = part


def pick_kernel(own, keep_far, panels_far, block):
    supernodes, _, rows_half, width = panels_far.shape
    parity = lax.axis_index("prow") % 2
    low = lax.broadcasted_iota(jnp.int32, (rows_half, width), 1) < width // 2
    block[parity] = own[...]
    for node in range(supernodes):
        lanes = slice(node * width, (node + 1) * width)
        value = packed(panels_far, node, low, parity) * keep_far[:, node : node + 1]
        block[1 - parity, :, lanes] = value.astype(jnp.bfloat16)


def merge_kernel(block, block_core, near, near_core, chip, first, second):
    carry = lax.axis_index("pcol") == 0
    _, rows_half, _ = block.shape
    for core, source in ((0, block_core), (1, block)):
        for x in range(2):
            rows = slice(x * rows_half, (x + 1) * rows_half)
            chip[core, rows] = source[x]
            first[core, rows] = jnp.where(carry, near[core, rows], source[x])
            second[core, rows] = jnp.where(carry, near_core[core, rows], source[x])


def product_kernel(near, near_core, far_0, far_1, held, out):
    count, _, rows_dev, lanes = held.shape
    depth = count * rows_dev
    for core, lefts in ((0, (near_core, far_0)), (1, (near, far_1))):
        right = held[:, core].reshape(depth, lanes)
        for far_or, left in enumerate(lefts):
            value = jnp.dot(left[...].reshape(2 * rows_dev, depth), right, preferred_element_type=jnp.float32)
            value = value.reshape(out.shape[1:])
            out[far_or] = value if core == 0 else out[far_or] + value


def left_kernel(panels, panels_far, panels_core, panels_far_core, out, rows):
    supernodes, _, rows_half, width = panels.shape
    for node in range(supernodes):
        for part in range(2):
            for far_or, (same, cross) in ((0, (panels, panels_core)), (1, (panels_far, panels_far_core))):
                rows[far_or, 0] = cross[node, part]
                rows[far_or, 1] = same[node, part]
            out[node, part] = rows[...].reshape(4 * rows_half, width).T


def columns_and_diagonal(orders, head, value_of, kept, left, own, send, diag, columns):
    supernodes, rows_half, width = own.shape
    rows_dev = 2 * rows_half
    some = supernodes * rows_half
    peak = jnp.zeros((1, 1), jnp.float32)
    for far_or in range(2):
        real, imag = value_of(far_or)
        for node in range(supernodes):
            lanes = slice(node * width, (node + 1) * width)
            keep = kept[far_or, :, node : node + 1]
            column = (-((real[:, lanes] + turned(imag[:, lanes])) * keep)).astype(jnp.bfloat16)
            columns[node, far_or] = column
            if far_or == 0:
                send[node * rows_half : (node + 1) * rows_half] = column[:rows_half]
                own[node] = column[rows_half:]
            else:
                peak = jnp.maximum(peak, largest(column.astype(jnp.float32)))
    level = level_of(peak, 13)
    factor = power(level, 0, STEP)
    send[3 * some :] = jnp.broadcast_to(level, (LEVEL_ROWS, width)).astype(jnp.bfloat16)
    for node in range(supernodes):
        column = (columns[node, 1].astype(jnp.float32) * factor).astype(jnp.bfloat16)
        start = some + node * rows_half
        send[start : start + rows_half] = column[:rows_half]
        send[start + some : start + some + rows_half] = column[rows_half:]
    values = []
    peak = jnp.zeros((1, 1), jnp.float32)
    for node in range(supernodes):
        both = jnp.dot(
            left[node].reshape(2 * width, 2 * rows_dev),
            columns[node].reshape(2 * rows_dev, width),
            preferred_element_type=jnp.float32,
        )
        values.append(both[:width] + turned(both[width:]))
        peak = jnp.maximum(peak, largest(values[-1]))
    level = level_of(peak, head + orders)
    factor = power(level, -orders, STEP)
    for node, value in enumerate(values):
        diag[node * width : (node + 1) * width] = value * factor
    diag[supernodes * width :] = jnp.broadcast_to(level, (LEVEL_ROWS, width))


def diagonal_kernel(orders, head, product, *refs):
    columns_and_diagonal(orders, head, lambda far_or: (product[far_or, 0], product[far_or, 1]), *refs)


def whole_kernel(orders, head, near, near_core, far_0, far_1, block_0, block_1, block_2, block_3, *refs):
    _, rows_dev, depth = near.shape
    blocks = (block_0, block_1, block_2, block_3)
    right = jnp.concatenate([block[core] for core in range(2) for block in blocks])

    def value_of(far_or):
        pair = ((near_core, near), (far_0, far_1))[far_or]
        both = jnp.concatenate([part[...].reshape(2 * rows_dev, depth) for part in pair], axis=1)
        value = jnp.dot(both, right, preferred_element_type=jnp.float32)
        return value[:rows_dev], value[rows_dev:]

    columns_and_diagonal(orders, head, value_of, *refs)


def unpack(near, far):
    parity = lax.axis_index("prow") % 2
    low = jnp.where(parity == 0, near, far)
    high = jnp.where(parity == 0, far, near)
    first = lax.broadcasted_iota(jnp.int32, near.shape, 1) < near.shape[1] // 2
    return jnp.where(first, low, swap_halves(high)), jnp.where(first, swap_halves(low), high)


def columns_kernel(own, own_core, other, other_core, out):
    supernodes, _, rows_half, width = out.shape
    first = lax.axis_index("pcol") == 0
    for node in range(supernodes):
        rows = slice(node * rows_half, (node + 1) * rows_half)
        near = jnp.where(first, own_core[rows].astype(jnp.float32), own[rows].astype(jnp.float32))
        far = jnp.where(first, other[rows].astype(jnp.float32), other_core[rows].astype(jnp.float32))
        real, imag = unpack(near, far)
        out[node, 0] = real.astype(jnp.bfloat16)
        out[node, 1] = imag.astype(jnp.bfloat16)


def final_kernel(orders, diag_inverse, mine, far, mine_core, far_core, out, value, done):
    supernodes, _, width, _ = out.shape
    first = lax.axis_index("pcol") == 0
    end = supernodes * width
    near_level = jnp.where(first, mine_core[end : end + 1], mine[end : end + 1])
    far_level = jnp.where(first, far_core[end : end + 1], far[end : end + 1])
    near_scale, far_scale = power(near_level, orders, -STEP), power(far_level, orders, -STEP)
    copies = [pltpu.make_async_copy(value.at[node], out.at[node], done.at[node]) for node in range(supernodes)]
    for node in range(supernodes):
        rows = slice(node * width, (node + 1) * width)
        near_value = jnp.where(first, mine_core[rows], mine[rows]) * near_scale
        far_value = jnp.where(first, far_core[rows], far[rows]) * far_scale
        real, imag = unpack(near_value, far_value)
        value[node, 0] = diag_inverse[node, 0].astype(jnp.float32) - real
        value[node, 1] = diag_inverse[node, 1].astype(jnp.float32) - imag
        copies[node].start()
    for copy in copies:
        copy.wait()


def solution(mesh):
    rows, cols = mesh.shape["prow"], mesh.shape["pcol"]

    def local(anc_inverse, panels, diag_inverse, structure):
        supernodes, _, rows_half, width = panels.shape
        half = width // 2
        groups = anc_inverse.shape[1]
        rows_dev = anc_inverse.shape[4]
        lanes = supernodes * width
        row_index = lax.axis_index("prow")
        col_index = lax.axis_index("pcol")
        here = row_index // 2
        bf16, f32 = jnp.bfloat16, jnp.float32

        panels = plain(panels)
        panels_far = plain(swap(panels, rows, cols, 1, 1))
        chip_shape = (2, rows_dev, lanes)
        shape = (2, rows_dev, groups * rows_half)
        near, panels, diag_inverse, keep, keep_far, own = call(
            first_kernel,
            [
                (shape, bf16),
                (panels.shape, bf16),
                (diag_inverse.shape, bf16),
                ((2, rows_dev, 128), f32),
                ((rows_half, 128), f32),
                ((rows_half, lanes), bf16),
            ],
            [pltpu.with_memory_space_constraint(v, pltpu.HBM) for v in (anc_inverse, panels, diag_inverse, structure)],
            [
                pltpu.VMEM(anc_inverse.shape, bf16),
                pltpu.VMEM(structure.shape, jnp.int32),
                pltpu.SemaphoreType.DMA((4,)),
            ],
            cost=12 << 20,
            space=HBM,
        )
        near_core = swap_core(near)
        panels_core = swap_core(panels)
        (block,) = call(pick_kernel, [((2, rows_half, lanes), bf16)], [own, keep_far, panels_far])
        if shape == chip_shape:
            chip, first, second = call(
                merge_kernel, [(chip_shape, bf16)] * 3, [block, swap_core(block), near, near_core]
            )
            far_0 = far_1 = None
        else:
            chip = first = second = jnp.stack([swap_core(block), block]).reshape(chip_shape)
            far_1 = swap(near, rows, cols, 1, 1)
            far_0 = swap_core(far_1)
        arrived = [swap(value, rows, cols, 1, mask) for value, mask in zip((first, second, chip), MASKS)]
        if far_0 is None:
            far_0, far_1 = swap_core(arrived[0]), swap_core(arrived[1])
        panels_far_core = swap_core(panels_far)
        (left,) = call(
            left_kernel,
            [((supernodes, 2, width, 2 * rows_dev), bf16)],
            [panels, panels_far, panels_core, panels_far_core],
            [pltpu.VMEM((2, cols, rows_half, width), bf16)],
        )
        orders = max(0, math.ceil(math.log2(groups * 2 * rows_half / 24)))
        head = 15 - int(math.log2(rows // 2))
        count = supernodes * width
        some = supernodes * rows_half
        outs = [
            ((supernodes, rows_half, width), bf16),
            ((3 * some + LEVEL_ROWS, width), bf16),
            ((count + LEVEL_ROWS, width), f32),
        ]
        sums = (2, 2, rows_dev, lanes)
        columns_scratch = pltpu.VMEM((supernodes, 2, rows_dev, width), bf16)
        lefts = [near, near_core, far_0, far_1]
        arrived = list(lax.optimization_barrier(tuple(arrived)))
        if rows == 8:
            own, send, diag = call(
                functools.partial(whole_kernel, orders, head),
                outs,
                lefts + [chip] + arrived + [keep, left],
                [columns_scratch],
            )
        else:
            held = jnp.stack([chip] + arrived)
            size = 8
            while size < rows:
                held = jnp.concatenate([held, swap(held, rows, cols, 1, size)])
                size *= 2
            (product,) = call(product_kernel, [(sums, f32)], lefts + [held])
            own, send, diag = call(
                functools.partial(diagonal_kernel, orders, head), outs, [product, keep, left], [columns_scratch]
            )
        f16 = jnp.float16
        term = diag.astype(f16)
        sent = swap_core(send)
        last = jnp.concatenate([sent[some:].astype(f16), term[2 * some + LEVEL_ROWS :]])
        last = jnp.where(col_index == 0, last, term)
        terms = [swap(v, rows, cols, 1, mask) for mask, v in zip(MASKS_SUM, (term, term, last))]
        wide = [t.astype(f32) for t in [term] + terms]
        levels = [t[count : count + 1] for t in wide]
        mine, first, second, third = [t[:count] * power(v, orders, -STEP) for t, v in zip(wide, levels)]
        total = (mine + first) + (second + third)
        level = functools.reduce(jnp.minimum, levels)
        size = 8
        while size < rows:
            other = swap(jnp.concatenate([total, jnp.broadcast_to(level, (8, width))]), rows, cols, 1, size)
            total, level = total + other[:count], jnp.minimum(level, other[count : count + 1])
            size *= 2
        total = total * power(level, -orders, STEP)
        mine = jnp.concatenate([total, jnp.broadcast_to(level, (LEVEL_ROWS, width))]).astype(f16)
        far = swap(mine, rows, cols, 2, 1)
        other = wide[3][: 2 * some] * power(wide[3][2 * some : 2 * some + 1], 0, -STEP)
        other = other.astype(bf16)
        (columns,) = call(
            columns_kernel,
            [((supernodes, 2, rows_half, width), bf16)],
            [own.reshape(some, width), sent[:some], other[:some], swap_core(other[some:])],
        )
        far_sent = far
        far_sent = after(far, columns)
        pieces = [v.astype(f32) for v in (mine, far, swap_core(mine), swap_core(far_sent))]
        (diag,) = call(
            functools.partial(final_kernel, orders),
            [((supernodes, 2, width, width), f32)],
            [diag_inverse] + pieces,
            [pltpu.VMEM((supernodes, 2, width, width), f32), pltpu.SemaphoreType.DMA((supernodes,))],
            out_space=HBM,
        )
        return columns, diag

    in_specs = (
        P("pole", None, "pcol", None, "prow"),
        P("pole", None, ("prow", "pcol"), None),
        P("pole", None, None, None),
        P(),
    )
    out_specs = (P("pole", None, ("prow", "pcol"), None), P("pole", None, None, None))
    return jax.shard_map(local, mesh=mesh, in_specs=in_specs, out_specs=out_specs, check_vma=False)
```

```python
import functools
import math

import jax
import jax.numpy as jnp
from jax import lax
from jax.experimental import pallas as pl
from jax.experimental.layout import Layout, with_layout_constraint
from jax.experimental.pallas import tpu as pltpu
from jax.sharding import PartitionSpec as P

AXES = ("prow", "pcol")
MASKS = (4, 2, 6)
MASKS_SUM = (2, 4, 6)
STEP, LEVELS, LEVEL_ROWS = 16, 5, 16
VMEM = pl.BlockSpec(memory_space=pltpu.VMEM)
HBM = pl.BlockSpec(memory_space=pltpu.HBM)


def steps_of(count):
    steps = [0] + [mask // 2 for mask in MASKS]
    while len(steps) < count:
        steps = steps + [step ^ len(steps) for step in steps]
    return steps


def swap(value, rows, cols, mask0, mask1):
    pairs = []
    for row in range(rows):
        for col in range(cols):
            mask = mask0 if col == 0 else mask1
            pairs.append((row * cols + col, (row ^ mask) * cols + col))
    return lax.ppermute(value, AXES, pairs)


def power(level, first, step):
    value = jnp.full(level.shape, 2.0**first, jnp.float32)
    for count in range(1, LEVELS + 1):
        value = jnp.where(level > count - 0.5, 2.0 ** (first + step * count), value)
    return value


def level_of(peak, head):
    level = jnp.zeros(peak.shape, jnp.float32)
    for count in range(1, LEVELS + 1):
        level += jnp.where(peak < 2.0 ** (head - STEP * count), 1.0, 0.0)
    return level


def largest(value):
    return jnp.max(jnp.max(jnp.abs(value), axis=0, keepdims=True), axis=1, keepdims=True)


def swap_core(value):
    return lax.ppermute(value, "pcol", [(0, 1), (1, 0)])


def after(value, *others):
    return lax.optimization_barrier((value,) + others)[0]


def plain(value):
    return with_layout_constraint(value, Layout(tuple(range(value.ndim))))


def call(kernel, outs, operands, scratch=(), cost=0, space=VMEM, out_space=VMEM, limit=0):
    shapes = [jax.ShapeDtypeStruct(shape, dtype) for shape, dtype in outs]
    size = sum(v.size * v.dtype.itemsize for v in list(operands) + shapes)
    return pl.pallas_call(
        kernel,
        out_shape=shapes,
        in_specs=[space] * len(operands),
        out_specs=[out_space] * len(shapes),
        scratch_shapes=list(scratch),
        cost_estimate=pl.CostEstimate(flops=0, bytes_accessed=cost or size, transcendentals=0),
        compiler_params=pltpu.CompilerParams(vmem_limit_bytes=limit or 2 * size + (4 << 20)),
    )(*operands)


def keep_rows(structure, node, start, count, width):
    blocks = structure.shape[1]
    row = start + lax.broadcasted_iota(jnp.int32, (count, blocks), 0)
    hit = row // width == lax.broadcasted_iota(jnp.int32, (count, blocks), 1)
    table = structure[node : node + 1, :].astype(jnp.float32)
    return jnp.sum(jnp.where(hit, table, 0.0), axis=1, keepdims=True)


def swap_halves(value):
    half = value.shape[-1] // 2
    return jnp.concatenate([value[:, half:], value[:, :half]], axis=-1)


def turned(value):
    lane = lax.broadcasted_iota(jnp.int32, value.shape, 1)
    other = swap_halves(value)
    return jnp.where(lane < value.shape[-1] // 2, -other, other)


def packed(source, node, low, parity):
    real = source[node, 0].astype(jnp.float32)
    imag = source[node, 1].astype(jnp.float32)
    left = jnp.where(low, real, swap_halves(imag))
    right = jnp.where(low, swap_halves(real), imag)
    return jnp.where(parity == 0, left, right)


def first_kernel(
    matrix_in, panels_in, diag_in, structure_in, across, panels, diag_inverse, keep, keep_far, own, matrix, structure, done
):
    pairs = ((panels_in, panels), (structure_in, structure), (matrix_in, matrix), (diag_in, diag_inverse))
    copies = [pltpu.make_async_copy(*pair, done.at[index]) for index, pair in enumerate(pairs)]
    for copy in copies:
        copy.start()
    for copy in copies:
        copy.wait()
    supernodes, _, rows_half, width = panels.shape
    groups, rows_dev = matrix.shape[1], matrix.shape[4]
    row_index, col_index = lax.axis_index("prow"), lax.axis_index("pcol")
    here = row_index // 2
    for part in range(2):
        pieces = [matrix[part, pl.ds(2 * (here ^ step), 2)] for step in steps_of(groups // 2)]
        across[part] = jnp.concatenate(pieces).reshape(groups * rows_half, rows_dev).T
    low = lax.broadcasted_iota(jnp.int32, (rows_half, width), 1) < width // 2
    for node in range(supernodes):
        lanes = slice(node * width, (node + 1) * width)
        for far_or in range(2):
            start = (row_index ^ far_or) * rows_dev
            value = keep_rows(structure, node, start, rows_dev, width)
            keep[far_or, :, node : node + 1] = value
            part = keep_rows(structure, node, start + col_index * rows_half, rows_half, width)
            if far_or == 0:
                own[:, lanes] = (packed(panels, node, low, row_index % 2) * part).astype(jnp.bfloat16)
            else:
                keep_far[:, node : node + 1] = part


def pick_kernel(own, keep_far, panels_far, block):
    supernodes, _, rows_half, width = panels_far.shape
    parity = lax.axis_index("prow") % 2
    low = lax.broadcasted_iota(jnp.int32, (rows_half, width), 1) < width // 2
    block[parity] = own[...]
    for node in range(supernodes):
        lanes = slice(node * width, (node + 1) * width)
        value = packed(panels_far, node, low, parity) * keep_far[:, node : node + 1]
        block[1 - parity, :, lanes] = value.astype(jnp.bfloat16)


def merge_kernel(block, block_core, near, near_core, chip, first, second):
    carry = lax.axis_index("pcol") == 0
    _, rows_half, _ = block.shape
    for core, source in ((0, block_core), (1, block)):
        for x in range(2):
            rows = slice(x * rows_half, (x + 1) * rows_half)
            chip[core, rows] = source[x]
            first[core, rows] = jnp.where(carry, near[core, rows], source[x])
            second[core, rows] = jnp.where(carry, near_core[core, rows], source[x])


def product_kernel(near, near_core, far_0, far_1, held, out):
    count, _, rows_dev, lanes = held.shape
    depth = count * rows_dev
    for core, lefts in ((0, (near_core, far_0)), (1, (near, far_1))):
        right = held[:, core].reshape(depth, lanes)
        for far_or, left in enumerate(lefts):
            value = jnp.dot(left[...].reshape(2 * rows_dev, depth), right, preferred_element_type=jnp.float32)
            value = value.reshape(out.shape[1:])
            out[far_or] = value if core == 0 else out[far_or] + value


def left_kernel(panels, panels_far, panels_core, panels_far_core, out, rows):
    supernodes, _, rows_half, width = panels.shape
    for node in range(supernodes):
        for part in range(2):
            for far_or, (same, cross) in ((0, (panels, panels_core)), (1, (panels_far, panels_far_core))):
                rows[far_or, 0] = cross[node, part]
                rows[far_or, 1] = same[node, part]
            out[node, part] = rows[...].reshape(4 * rows_half, width).T


def columns_and_diagonal(orders, head, value_of, kept, left, own, send, diag, columns):
    supernodes, rows_half, width = own.shape
    rows_dev = 2 * rows_half
    some = supernodes * rows_half
    peaks = []
    for far_or in range(2):
        real, imag = value_of(far_or)
        for node in range(supernodes):
            lanes = slice(node * width, (node + 1) * width)
            keep = kept[far_or, :, node : node + 1]
            column = (-((real[:, lanes] + turned(imag[:, lanes])) * keep)).astype(jnp.bfloat16)
            columns[node, far_or] = column
            if far_or == 0:
                send[node * rows_half : (node + 1) * rows_half] = column[:rows_half]
                own[node] = column[rows_half:]
            else:
                peaks.append(jnp.abs(column.astype(jnp.float32)))
    level = level_of(largest(functools.reduce(jnp.maximum, peaks)), 13)
    factor = power(level, 0, STEP)
    send[3 * some :] = jnp.broadcast_to(level, (LEVEL_ROWS, width)).astype(jnp.bfloat16)
    for node in range(supernodes):
        column = (columns[node, 1].astype(jnp.float32) * factor).astype(jnp.bfloat16)
        start = some + node * rows_half
        send[start : start + rows_half] = column[:rows_half]
        send[start + some : start + some + rows_half] = column[rows_half:]
    values = []
    for node in range(supernodes):
        both = jnp.dot(
            left[node].reshape(2 * width, 2 * rows_dev),
            columns[node].reshape(2 * rows_dev, width),
            preferred_element_type=jnp.float32,
        )
        values.append(both[:width] + turned(both[width:]))
    level = level_of(largest(functools.reduce(jnp.maximum, [jnp.abs(value) for value in values])), head + orders)
    factor = power(level, -orders, STEP)
    for node, value in enumerate(values):
        diag[node * width : (node + 1) * width] = value * factor
    diag[supernodes * width :] = jnp.broadcast_to(level, (LEVEL_ROWS, width))


def diagonal_kernel(orders, head, product, *refs):
    columns_and_diagonal(orders, head, lambda far_or: (product[far_or, 0], product[far_or, 1]), *refs)


def whole_kernel(orders, head, near, near_core, far_0, far_1, block_0, block_1, block_2, block_3, *refs):
    _, rows_dev, depth = near.shape
    blocks = (block_0, block_1, block_2, block_3)
    right = jnp.concatenate([block[core] for core in range(2) for block in blocks])

    def value_of(far_or):
        pair = ((near_core, near), (far_0, far_1))[far_or]
        both = jnp.concatenate([part[...].reshape(2 * rows_dev, depth) for part in pair], axis=1)
        value = jnp.dot(both, right, preferred_element_type=jnp.float32)
        return value[:rows_dev], value[rows_dev:]

    columns_and_diagonal(orders, head, value_of, *refs)


def unpack(near, far):
    parity = lax.axis_index("prow") % 2
    low = jnp.where(parity == 0, near, far)
    high = jnp.where(parity == 0, far, near)
    first = lax.broadcasted_iota(jnp.int32, near.shape, 1) < near.shape[1] // 2
    return jnp.where(first, low, swap_halves(high)), jnp.where(first, swap_halves(low), high)


def columns_kernel(own, own_core, other, other_core, out):
    supernodes, _, rows_half, width = out.shape
    first = lax.axis_index("pcol") == 0
    for node in range(supernodes):
        rows = slice(node * rows_half, (node + 1) * rows_half)
        near = jnp.where(first, own_core[rows].astype(jnp.float32), own[rows].astype(jnp.float32))
        far = jnp.where(first, other[rows].astype(jnp.float32), other_core[rows].astype(jnp.float32))
        real, imag = unpack(near, far)
        out[node, 0] = real.astype(jnp.bfloat16)
        out[node, 1] = imag.astype(jnp.bfloat16)


def final_kernel(orders, diag_inverse, mine, far, mine_core, far_core, out, value, done):
    supernodes, _, width, _ = out.shape
    first = lax.axis_index("pcol") == 0
    end = supernodes * width
    near_level = jnp.where(first, mine_core[end : end + 1], mine[end : end + 1])
    far_level = jnp.where(first, far_core[end : end + 1], far[end : end + 1])
    near_scale, far_scale = power(near_level, orders, -STEP), power(far_level, orders, -STEP)
    copies = [pltpu.make_async_copy(value.at[node], out.at[node], done.at[node]) for node in range(supernodes)]
    for node in range(supernodes):
        rows = slice(node * width, (node + 1) * width)
        near_value = jnp.where(first, mine_core[rows], mine[rows]) * near_scale
        far_value = jnp.where(first, far_core[rows], far[rows]) * far_scale
        real, imag = unpack(near_value, far_value)
        value[node, 0] = diag_inverse[node, 0].astype(jnp.float32) - real
        value[node, 1] = diag_inverse[node, 1].astype(jnp.float32) - imag
        copies[node].start()
    for copy in copies:
        copy.wait()


def solution(mesh):
    rows, cols = mesh.shape["prow"], mesh.shape["pcol"]

    def local(anc_inverse, panels, diag_inverse, structure):
        supernodes, _, rows_half, width = panels.shape
        half = width // 2
        groups = anc_inverse.shape[1]
        rows_dev = anc_inverse.shape[4]
        lanes = supernodes * width
        row_index = lax.axis_index("prow")
        col_index = lax.axis_index("pcol")
        here = row_index // 2
        bf16, f32 = jnp.bfloat16, jnp.float32

        panels = plain(panels)
        panels_far = plain(swap(panels, rows, cols, 1, 1))
        chip_shape = (2, rows_dev, lanes)
        shape = (2, rows_dev, groups * rows_half)
        near, panels, diag_inverse, keep, keep_far, own = call(
            first_kernel,
            [
                (shape, bf16),
                (panels.shape, bf16),
                (diag_inverse.shape, bf16),
                ((2, rows_dev, 128), f32),
                ((rows_half, 128), f32),
                ((rows_half, lanes), bf16),
            ],
            [pltpu.with_memory_space_constraint(v, pltpu.HBM) for v in (anc_inverse, panels, diag_inverse, structure)],
            [
                pltpu.VMEM(anc_inverse.shape, bf16),
                pltpu.VMEM(structure.shape, jnp.int32),
                pltpu.SemaphoreType.DMA((4,)),
            ],
            cost=12 << 20,
            space=HBM,
        )
        near_core = swap_core(near)
        panels_core = swap_core(panels)
        (block,) = call(pick_kernel, [((2, rows_half, lanes), bf16)], [own, keep_far, panels_far])
        if shape == chip_shape:
            chip, first, second = call(
                merge_kernel, [(chip_shape, bf16)] * 3, [block, swap_core(block), near, near_core]
            )
            far_0 = far_1 = None
        else:
            chip = first = second = jnp.stack([swap_core(block), block]).reshape(chip_shape)
            far_1 = swap(near, rows, cols, 1, 1)
            far_0 = swap_core(far_1)
        arrived = [swap(value, rows, cols, 1, mask) for value, mask in zip((first, second, chip), MASKS)]
        if far_0 is None:
            far_0, far_1 = swap_core(arrived[0]), swap_core(arrived[1])
        panels_far_core = swap_core(panels_far)
        (left,) = call(
            left_kernel,
            [((supernodes, 2, width, 2 * rows_dev), bf16)],
            [panels, panels_far, panels_core, panels_far_core],
            [pltpu.VMEM((2, cols, rows_half, width), bf16)],
        )
        orders = max(0, math.ceil(math.log2(groups * 2 * rows_half / 24)))
        head = 15 - int(math.log2(rows // 2))
        count = supernodes * width
        some = supernodes * rows_half
        outs = [
            ((supernodes, rows_half, width), bf16),
            ((3 * some + LEVEL_ROWS, width), bf16),
            ((count + LEVEL_ROWS, width), f32),
        ]
        sums = (2, 2, rows_dev, lanes)
        columns_scratch = pltpu.VMEM((supernodes, 2, rows_dev, width), bf16)
        lefts = [near, near_core, far_0, far_1]
        arrived = list(lax.optimization_barrier(tuple(arrived)))
        if rows == 8:
            own, send, diag = call(
                functools.partial(whole_kernel, orders, head),
                outs,
                lefts + [chip] + arrived + [keep, left],
                [columns_scratch],
            )
        else:
            held = jnp.stack([chip] + arrived)
            size = 8
            while size < rows:
                held = jnp.concatenate([held, swap(held, rows, cols, 1, size)])
                size *= 2
            (product,) = call(product_kernel, [(sums, f32)], lefts + [held])
            own, send, diag = call(
                functools.partial(diagonal_kernel, orders, head), outs, [product, keep, left], [columns_scratch]
            )
        f16 = jnp.float16
        term = diag.astype(f16)
        sent = swap_core(send)
        last = jnp.concatenate([sent[some:].astype(f16), term[2 * some + LEVEL_ROWS :]])
        last = jnp.where(col_index == 0, last, term)
        terms = [swap(v, rows, cols, 1, mask) for mask, v in zip(MASKS_SUM, (term, term, last))]
        wide = [t.astype(f32) for t in [term] + terms]
        levels = [t[count : count + 1] for t in wide]
        mine, first, second, third = [t * power(v, orders, -STEP) for t, v in zip(wide, levels)]
        total = (mine + first) + (second + third)
        level = functools.reduce(jnp.minimum, levels)
        is_level = lax.broadcasted_iota(jnp.int32, total.shape, 0) >= count
        size = 8
        while size < rows:
            other = swap(jnp.where(is_level, level, total), rows, cols, 1, size)
            total, level = total + other, jnp.minimum(level, other[count : count + 1])
            size *= 2
        mine = jnp.where(is_level, level, total * power(level, -orders, STEP)).astype(f16)
        far = swap(mine, rows, cols, 2, 1)
        other = wide[3][: 2 * some] * power(wide[3][2 * some : 2 * some + 1], 0, -STEP)
        other = other.astype(bf16)
        (columns,) = call(
            columns_kernel,
            [((supernodes, 2, rows_half, width), bf16)],
            [own.reshape(some, width), sent[:some], other[:some], swap_core(other[some:])],
        )
        far_sent = far
        far_sent = after(far, columns)
        pieces = [v.astype(f32) for v in (mine, far, swap_core(mine), swap_core(far_sent))]
        (diag,) = call(
            functools.partial(final_kernel, orders),
            [((supernodes, 2, width, width), f32)],
            [diag_inverse] + pieces,
            [pltpu.VMEM((supernodes, 2, width, width), f32), pltpu.SemaphoreType.DMA((supernodes,))],
            out_space=HBM,
        )
        return columns, diag

    in_specs = (
        P("pole", None, "pcol", None, "prow"),
        P("pole", None, ("prow", "pcol"), None),
        P("pole", None, None, None),
        P(),
    )
    out_specs = (P("pole", None, ("prow", "pcol"), None), P("pole", None, None, None))
    return jax.shard_map(local, mesh=mesh, in_specs=in_specs, out_specs=out_specs, check_vma=False)
```

```python
import functools
import math

import jax
import jax.numpy as jnp
from jax import lax
from jax.experimental import pallas as pl
from jax.experimental.layout import Layout, with_layout_constraint
from jax.experimental.pallas import tpu as pltpu
from jax.sharding import PartitionSpec as P

AXES = ("prow", "pcol")
MASKS = (4, 2, 6)
MASKS_SUM = (2, 4, 6)
STEP, LEVELS, LEVEL_ROWS = 16, 5, 16
VMEM = pl.BlockSpec(memory_space=pltpu.VMEM)
HBM = pl.BlockSpec(memory_space=pltpu.HBM)


def steps_of(count):
    steps = [0] + [mask // 2 for mask in MASKS]
    while len(steps) < count:
        steps = steps + [step ^ len(steps) for step in steps]
    return steps


def swap(value, rows, cols, mask0, mask1):
    pairs = []
    for row in range(rows):
        for col in range(cols):
            mask = mask0 if col == 0 else mask1
            pairs.append((row * cols + col, (row ^ mask) * cols + col))
    return lax.ppermute(value, AXES, pairs)


def power(level, first, step):
    value = jnp.full(level.shape, 2.0**first, jnp.float32)
    for count in range(1, LEVELS + 1):
        value = jnp.where(level > count - 0.5, 2.0 ** (first + step * count), value)
    return value


def level_of(peak, head):
    level = jnp.zeros(peak.shape, jnp.float32)
    for count in range(1, LEVELS + 1):
        level += jnp.where(peak < 2.0 ** (head - STEP * count), 1.0, 0.0)
    return level


def largest(value):
    return jnp.max(jnp.max(jnp.abs(value), axis=0, keepdims=True), axis=1, keepdims=True)


def swap_core(value):
    return lax.ppermute(value, "pcol", [(0, 1), (1, 0)])


def after(value, *others):
    return lax.optimization_barrier((value,) + others)[0]


def plain(value):
    return with_layout_constraint(value, Layout(tuple(range(value.ndim))))


def call(kernel, outs, operands, scratch=(), cost=0, space=VMEM, out_space=VMEM, limit=0):
    shapes = [jax.ShapeDtypeStruct(shape, dtype) for shape, dtype in outs]
    size = sum(v.size * v.dtype.itemsize for v in list(operands) + shapes)
    return pl.pallas_call(
        kernel,
        out_shape=shapes,
        in_specs=[space] * len(operands),
        out_specs=[out_space] * len(shapes),
        scratch_shapes=list(scratch),
        cost_estimate=pl.CostEstimate(flops=0, bytes_accessed=cost or size, transcendentals=0),
        compiler_params=pltpu.CompilerParams(vmem_limit_bytes=limit or 2 * size + (4 << 20)),
    )(*operands)


def keep_rows(structure, node, start, count, width):
    blocks = structure.shape[1]
    row = start + lax.broadcasted_iota(jnp.int32, (count, blocks), 0)
    hit = row // width == lax.broadcasted_iota(jnp.int32, (count, blocks), 1)
    table = structure[node : node + 1, :].astype(jnp.float32)
    return jnp.sum(jnp.where(hit, table, 0.0), axis=1, keepdims=True)


def swap_halves(value):
    half = value.shape[-1] // 2
    return jnp.concatenate([value[:, half:], value[:, :half]], axis=-1)


def turned(value):
    lane = lax.broadcasted_iota(jnp.int32, value.shape, 1)
    other = swap_halves(value)
    return jnp.where(lane < value.shape[-1] // 2, -other, other)


def packed(source, node, low, parity):
    real = source[node, 0].astype(jnp.float32)
    imag = source[node, 1].astype(jnp.float32)
    left = jnp.where(low, real, swap_halves(imag))
    right = jnp.where(low, swap_halves(real), imag)
    return jnp.where(parity == 0, left, right)


def first_kernel(
    matrix_in, panels_in, diag_in, structure_in, across, panels, diag_inverse, keep, keep_far, own, matrix, structure, done
):
    pairs = ((panels_in, panels), (structure_in, structure), (matrix_in, matrix), (diag_in, diag_inverse))
    copies = [pltpu.make_async_copy(*pair, done.at[index]) for index, pair in enumerate(pairs)]
    for copy in copies:
        copy.start()
    for copy in copies:
        copy.wait()
    supernodes, _, rows_half, width = panels.shape
    groups, rows_dev = matrix.shape[1], matrix.shape[4]
    row_index, col_index = lax.axis_index("prow"), lax.axis_index("pcol")
    here = row_index // 2
    for part in range(2):
        pieces = [matrix[part, pl.ds(2 * (here ^ step), 2)] for step in steps_of(groups // 2)]
        across[part] = jnp.concatenate(pieces).reshape(groups * rows_half, rows_dev).T
    low = lax.broadcasted_iota(jnp.int32, (rows_half, width), 1) < width // 2
    for node in range(supernodes):
        lanes = slice(node * width, (node + 1) * width)
        for far_or in range(2):
            start = (row_index ^ far_or) * rows_dev
            value = keep_rows(structure, node, start, rows_dev, width)
            keep[far_or, :, node : node + 1] = value
            part = keep_rows(structure, node, start + col_index * rows_half, rows_half, width)
            if far_or == 0:
                own[:, lanes] = (packed(panels, node, low, row_index % 2) * part).astype(jnp.bfloat16)
            else:
                keep_far[:, node : node + 1] = part


def pick_kernel(own, keep_far, panels_far, block):
    supernodes, _, rows_half, width = panels_far.shape
    parity = lax.axis_index("prow") % 2
    low = lax.broadcasted_iota(jnp.int32, (rows_half, width), 1) < width // 2
    block[parity] = own[...]
    for node in range(supernodes):
        lanes = slice(node * width, (node + 1) * width)
        value = packed(panels_far, node, low, parity) * keep_far[:, node : node + 1]
        block[1 - parity, :, lanes] = value.astype(jnp.bfloat16)


def merge_kernel(block, block_core, near, near_core, chip, first, second):
    carry = lax.axis_index("pcol") == 0
    _, rows_half, _ = block.shape
    for core, source in ((0, block_core), (1, block)):
        for x in range(2):
            rows = slice(x * rows_half, (x + 1) * rows_half)
            chip[core, rows] = source[x]
            first[core, rows] = jnp.where(carry, near[core, rows], source[x])
            second[core, rows] = jnp.where(carry, near_core[core, rows], source[x])


def product_kernel(near, near_core, far_0, far_1, held, out):
    count, _, rows_dev, lanes = held.shape
    depth = count * rows_dev
    for core, lefts in ((0, (near_core, far_0)), (1, (near, far_1))):
        right = held[:, core].reshape(depth, lanes)
        for far_or, left in enumerate(lefts):
            value = jnp.dot(left[...].reshape(2 * rows_dev, depth), right, preferred_element_type=jnp.float32)
            value = value.reshape(out.shape[1:])
            out[far_or] = value if core == 0 else out[far_or] + value


def left_kernel(panels, panels_far, panels_core, panels_far_core, out, rows):
    supernodes, _, rows_half, width = panels.shape
    for node in range(supernodes):
        for part in range(2):
            for far_or, (same, cross) in ((0, (panels, panels_core)), (1, (panels_far, panels_far_core))):
                rows[far_or, 0] = cross[node, part]
                rows[far_or, 1] = same[node, part]
            out[node, part] = rows[...].reshape(4 * rows_half, width).T


def columns_and_diagonal(orders, head, value_of, kept, left, own, send, diag, columns):
    supernodes, rows_half, width = own.shape
    rows_dev = 2 * rows_half
    some = supernodes * rows_half
    peaks = []
    for far_or in range(2):
        real, imag = value_of(far_or)
        for node in range(supernodes):
            lanes = slice(node * width, (node + 1) * width)
            keep = kept[far_or, :, node : node + 1]
            column = (-((real[:, lanes] + turned(imag[:, lanes])) * keep)).astype(jnp.bfloat16)
            columns[node, far_or] = column
            if far_or == 0:
                send[node * rows_half : (node + 1) * rows_half] = column[:rows_half]
                own[node] = column[rows_half:]
            else:
                peaks.append(jnp.abs(column.astype(jnp.float32)))
    level = level_of(largest(functools.reduce(jnp.maximum, peaks)), 13)
    factor = power(level, 0, STEP)
    send[3 * some :] = jnp.broadcast_to(level, (LEVEL_ROWS, width)).astype(jnp.bfloat16)
    for node in range(supernodes):
        column = (columns[node, 1].astype(jnp.float32) * factor).astype(jnp.bfloat16)
        start = some + node * rows_half
        send[start : start + rows_half] = column[:rows_half]
        send[start + some : start + some + rows_half] = column[rows_half:]
    values = []
    for node in range(supernodes):
        both = jnp.dot(
            left[node].reshape(2 * width, 2 * rows_dev),
            columns[node].reshape(2 * rows_dev, width),
            preferred_element_type=jnp.float32,
        )
        values.append(both[:width] + turned(both[width:]))
    for node, value in enumerate(values):
        diag[node * width : (node + 1) * width] = value
    level = level_of(largest(functools.reduce(jnp.maximum, [jnp.abs(value) for value in values])), head + orders)
    diag[supernodes * width :] = jnp.broadcast_to(level, (LEVEL_ROWS, width))


def diagonal_kernel(orders, head, product, *refs):
    columns_and_diagonal(orders, head, lambda far_or: (product[far_or, 0], product[far_or, 1]), *refs)


def whole_kernel(orders, head, near, near_core, far_0, far_1, block_0, block_1, block_2, block_3, *refs):
    _, rows_dev, depth = near.shape
    blocks = (block_0, block_1, block_2, block_3)
    right = jnp.concatenate([block[core] for core in range(2) for block in blocks])

    def value_of(far_or):
        pair = ((near_core, near), (far_0, far_1))[far_or]
        both = jnp.concatenate([part[...].reshape(2 * rows_dev, depth) for part in pair], axis=1)
        value = jnp.dot(both, right, preferred_element_type=jnp.float32)
        return value[:rows_dev], value[rows_dev:]

    columns_and_diagonal(orders, head, value_of, *refs)


def unpack(near, far):
    parity = lax.axis_index("prow") % 2
    low = jnp.where(parity == 0, near, far)
    high = jnp.where(parity == 0, far, near)
    first = lax.broadcasted_iota(jnp.int32, near.shape, 1) < near.shape[1] // 2
    return jnp.where(first, low, swap_halves(high)), jnp.where(first, swap_halves(low), high)


def columns_kernel(own, own_core, other, other_core, out):
    supernodes, _, rows_half, width = out.shape
    first = lax.axis_index("pcol") == 0
    for node in range(supernodes):
        rows = slice(node * rows_half, (node + 1) * rows_half)
        near = jnp.where(first, own_core[rows].astype(jnp.float32), own[rows].astype(jnp.float32))
        far = jnp.where(first, other[rows].astype(jnp.float32), other_core[rows].astype(jnp.float32))
        real, imag = unpack(near, far)
        out[node, 0] = real.astype(jnp.bfloat16)
        out[node, 1] = imag.astype(jnp.bfloat16)


def final_kernel(orders, diag_inverse, mine, far, mine_core, far_core, out, value, done):
    supernodes, _, width, _ = out.shape
    first = lax.axis_index("pcol") == 0
    end = supernodes * width
    near_level = jnp.where(first, mine_core[end : end + 1], mine[end : end + 1])
    far_level = jnp.where(first, far_core[end : end + 1], far[end : end + 1])
    near_scale, far_scale = power(near_level, orders, -STEP), power(far_level, orders, -STEP)
    copies = [pltpu.make_async_copy(value.at[node], out.at[node], done.at[node]) for node in range(supernodes)]
    for node in range(supernodes):
        rows = slice(node * width, (node + 1) * width)
        near_value = jnp.where(first, mine_core[rows], mine[rows]) * near_scale
        far_value = jnp.where(first, far_core[rows], far[rows]) * far_scale
        real, imag = unpack(near_value, far_value)
        value[node, 0] = diag_inverse[node, 0].astype(jnp.float32) - real
        value[node, 1] = diag_inverse[node, 1].astype(jnp.float32) - imag
        copies[node].start()
    for copy in copies:
        copy.wait()


def solution(mesh):
    rows, cols = mesh.shape["prow"], mesh.shape["pcol"]

    def local(anc_inverse, panels, diag_inverse, structure):
        supernodes, _, rows_half, width = panels.shape
        half = width // 2
        groups = anc_inverse.shape[1]
        rows_dev = anc_inverse.shape[4]
        lanes = supernodes * width
        row_index = lax.axis_index("prow")
        col_index = lax.axis_index("pcol")
        here = row_index // 2
        bf16, f32 = jnp.bfloat16, jnp.float32

        panels = plain(panels)
        panels_far = plain(swap(panels, rows, cols, 1, 1))
        chip_shape = (2, rows_dev, lanes)
        shape = (2, rows_dev, groups * rows_half)
        near, panels, diag_inverse, keep, keep_far, own = call(
            first_kernel,
            [
                (shape, bf16),
                (panels.shape, bf16),
                (diag_inverse.shape, bf16),
                ((2, rows_dev, 128), f32),
                ((rows_half, 128), f32),
                ((rows_half, lanes), bf16),
            ],
            [pltpu.with_memory_space_constraint(v, pltpu.HBM) for v in (anc_inverse, panels, diag_inverse, structure)],
            [
                pltpu.VMEM(anc_inverse.shape, bf16),
                pltpu.VMEM(structure.shape, jnp.int32),
                pltpu.SemaphoreType.DMA((4,)),
            ],
            cost=12 << 20,
            space=HBM,
        )
        near_core = swap_core(near)
        panels_core = swap_core(panels)
        (block,) = call(pick_kernel, [((2, rows_half, lanes), bf16)], [own, keep_far, panels_far])
        if shape == chip_shape:
            chip, first, second = call(
                merge_kernel, [(chip_shape, bf16)] * 3, [block, swap_core(block), near, near_core]
            )
            far_0 = far_1 = None
        else:
            chip = first = second = jnp.stack([swap_core(block), block]).reshape(chip_shape)
            far_1 = swap(near, rows, cols, 1, 1)
            far_0 = swap_core(far_1)
        arrived = [swap(value, rows, cols, 1, mask) for value, mask in zip((first, second, chip), MASKS)]
        if far_0 is None:
            far_0, far_1 = swap_core(arrived[0]), swap_core(arrived[1])
        panels_far_core = swap_core(panels_far)
        (left,) = call(
            left_kernel,
            [((supernodes, 2, width, 2 * rows_dev), bf16)],
            [panels, panels_far, panels_core, panels_far_core],
            [pltpu.VMEM((2, cols, rows_half, width), bf16)],
        )
        orders = max(0, math.ceil(math.log2(groups * 2 * rows_half / 24)))
        head = 15 - int(math.log2(rows // 2))
        count = supernodes * width
        some = supernodes * rows_half
        outs = [
            ((supernodes, rows_half, width), bf16),
            ((3 * some + LEVEL_ROWS, width), bf16),
            ((count + LEVEL_ROWS, width), f32),
        ]
        sums = (2, 2, rows_dev, lanes)
        columns_scratch = pltpu.VMEM((supernodes, 2, rows_dev, width), bf16)
        lefts = [near, near_core, far_0, far_1]
        arrived = list(lax.optimization_barrier(tuple(arrived)))
        if rows == 8:
            own, send, diag = call(
                functools.partial(whole_kernel, orders, head),
                outs,
                lefts + [chip] + arrived + [keep, left],
                [columns_scratch],
            )
        else:
            held = jnp.stack([chip] + arrived)
            size = 8
            while size < rows:
                held = jnp.concatenate([held, swap(held, rows, cols, 1, size)])
                size *= 2
            (product,) = call(product_kernel, [(sums, f32)], lefts + [held])
            own, send, diag = call(
                functools.partial(diagonal_kernel, orders, head), outs, [product, keep, left], [columns_scratch]
            )
        f16 = jnp.float16
        is_level = lax.broadcasted_iota(jnp.int32, diag.shape, 0) >= count
        level = diag[count : count + 1]
        term = jnp.where(is_level, level, diag * power(level, -orders, STEP)).astype(f16)
        sent = swap_core(send)
        last = jnp.concatenate([sent[some:].astype(f16), term[2 * some + LEVEL_ROWS :]])
        last = jnp.where(col_index == 0, last, term)
        terms = [swap(v, rows, cols, 1, mask) for mask, v in zip(MASKS_SUM, (term, term, last))]
        wide = [t.astype(f32) for t in [term] + terms]
        levels = [t[count : count + 1] for t in wide]
        mine, first, second, third = [t * power(v, orders, -STEP) for t, v in zip(wide, levels)]
        total = (mine + first) + (second + third)
        level = functools.reduce(jnp.minimum, levels)
        size = 8
        while size < rows:
            other = swap(jnp.where(is_level, level, total), rows, cols, 1, size)
            total, level = total + other, jnp.minimum(level, other[count : count + 1])
            size *= 2
        mine = jnp.where(is_level, level, total * power(level, -orders, STEP)).astype(f16)
        far = swap(mine, rows, cols, 2, 1)
        other = wide[3][: 2 * some] * power(wide[3][2 * some : 2 * some + 1], 0, -STEP)
        other = other.astype(bf16)
        (columns,) = call(
            columns_kernel,
            [((supernodes, 2, rows_half, width), bf16)],
            [own.reshape(some, width), sent[:some], other[:some], swap_core(other[some:])],
        )
        far_sent = far
        far_sent = after(far, columns)
        pieces = [v.astype(f32) for v in (mine, far, swap_core(mine), swap_core(far_sent))]
        (diag,) = call(
            functools.partial(final_kernel, orders),
            [((supernodes, 2, width, width), f32)],
            [diag_inverse] + pieces,
            [pltpu.VMEM((supernodes, 2, width, width), f32), pltpu.SemaphoreType.DMA((supernodes,))],
            out_space=HBM,
        )
        return columns, diag

    in_specs = (
        P("pole", None, "pcol", None, "prow"),
        P("pole", None, ("prow", "pcol"), None),
        P("pole", None, None, None),
        P(),
    )
    out_specs = (P("pole", None, ("prow", "pcol"), None), P("pole", None, None, None))
    return jax.shard_map(local, mesh=mesh, in_specs=in_specs, out_specs=out_specs, check_vma=False)
```

```python
import functools
import math

import jax
import jax.numpy as jnp
from jax import lax
from jax.experimental import pallas as pl
from jax.experimental.layout import Layout, with_layout_constraint
from jax.experimental.pallas import tpu as pltpu
from jax.sharding import PartitionSpec as P

AXES = ("prow", "pcol")
MASKS = (4, 2, 6)
MASKS_SUM = (6, 2, 4)
STEP, LEVELS, LEVEL_ROWS = 16, 5, 16
VMEM = pl.BlockSpec(memory_space=pltpu.VMEM)
HBM = pl.BlockSpec(memory_space=pltpu.HBM)


def steps_of(count):
    steps = [0] + [mask // 2 for mask in MASKS]
    while len(steps) < count:
        steps = steps + [step ^ len(steps) for step in steps]
    return steps


def swap(value, rows, cols, mask0, mask1):
    pairs = []
    for row in range(rows):
        for col in range(cols):
            mask = mask0 if col == 0 else mask1
            pairs.append((row * cols + col, (row ^ mask) * cols + col))
    return lax.ppermute(value, AXES, pairs)


def power(level, first, step):
    value = jnp.full(level.shape, 2.0**first, jnp.float32)
    for count in range(1, LEVELS + 1):
        value = jnp.where(level > count - 0.5, 2.0 ** (first + step * count), value)
    return value


def level_of(peak, head):
    level = jnp.zeros(peak.shape, jnp.float32)
    for count in range(1, LEVELS + 1):
        level += jnp.where(peak < 2.0 ** (head - STEP * count), 1.0, 0.0)
    return level


def largest(value):
    return jnp.max(jnp.max(jnp.abs(value), axis=0, keepdims=True), axis=1, keepdims=True)


def swap_core(value):
    return lax.ppermute(value, "pcol", [(0, 1), (1, 0)])


def after(value, *others):
    return lax.optimization_barrier((value,) + others)[0]


def plain(value):
    return with_layout_constraint(value, Layout(tuple(range(value.ndim))))


def call(kernel, outs, operands, scratch=(), cost=0, space=VMEM, out_space=VMEM, limit=0):
    shapes = [jax.ShapeDtypeStruct(shape, dtype) for shape, dtype in outs]
    size = sum(v.size * v.dtype.itemsize for v in list(operands) + shapes)
    return pl.pallas_call(
        kernel,
        out_shape=shapes,
        in_specs=[space] * len(operands),
        out_specs=[out_space] * len(shapes),
        scratch_shapes=list(scratch),
        cost_estimate=pl.CostEstimate(flops=0, bytes_accessed=cost or size, transcendentals=0),
        compiler_params=pltpu.CompilerParams(vmem_limit_bytes=limit or 2 * size + (4 << 20)),
    )(*operands)


def keep_rows(structure, node, start, count, width):
    blocks = structure.shape[1]
    row = start + lax.broadcasted_iota(jnp.int32, (count, blocks), 0)
    hit = row // width == lax.broadcasted_iota(jnp.int32, (count, blocks), 1)
    table = structure[node : node + 1, :].astype(jnp.float32)
    return jnp.sum(jnp.where(hit, table, 0.0), axis=1, keepdims=True)


def swap_halves(value):
    half = value.shape[-1] // 2
    return jnp.concatenate([value[:, half:], value[:, :half]], axis=-1)


def turned(value):
    lane = lax.broadcasted_iota(jnp.int32, value.shape, 1)
    other = swap_halves(value)
    return jnp.where(lane < value.shape[-1] // 2, -other, other)


def packed(source, node, low, parity):
    real = source[node, 0].astype(jnp.float32)
    imag = source[node, 1].astype(jnp.float32)
    left = jnp.where(low, real, swap_halves(imag))
    right = jnp.where(low, swap_halves(real), imag)
    return jnp.where(parity == 0, left, right)


def first_kernel(
    matrix_in, panels_in, diag_in, structure_in, across, panels, diag_inverse, keep, keep_far, own, matrix, structure, done
):
    pairs = ((panels_in, panels), (structure_in, structure), (matrix_in, matrix), (diag_in, diag_inverse))
    copies = [pltpu.make_async_copy(*pair, done.at[index]) for index, pair in enumerate(pairs)]
    for copy in copies:
        copy.start()
    for copy in copies:
        copy.wait()
    supernodes, _, rows_half, width = panels.shape
    groups, rows_dev = matrix.shape[1], matrix.shape[4]
    row_index, col_index = lax.axis_index("prow"), lax.axis_index("pcol")
    here = row_index // 2
    for part in range(2):
        pieces = [matrix[part, pl.ds(2 * (here ^ step), 2)] for step in steps_of(groups // 2)]
        across[part] = jnp.concatenate(pieces).reshape(groups * rows_half, rows_dev).T
    low = lax.broadcasted_iota(jnp.int32, (rows_half, width), 1) < width // 2
    for node in range(supernodes):
        lanes = slice(node * width, (node + 1) * width)
        for far_or in range(2):
            start = (row_index ^ far_or) * rows_dev
            value = keep_rows(structure, node, start, rows_dev, width)
            keep[far_or, :, node : node + 1] = value
            part = keep_rows(structure, node, start + col_index * rows_half, rows_half, width)
            if far_or == 0:
                own[:, lanes] = (packed(panels, node, low, row_index % 2) * part).astype(jnp.bfloat16)
            else:
                keep_far[:, node : node + 1] = part


def pick_kernel(own, keep_far, panels_far, block):
    supernodes, _, rows_half, width = panels_far.shape
    parity = lax.axis_index("prow") % 2
    low = lax.broadcasted_iota(jnp.int32, (rows_half, width), 1) < width // 2
    block[parity] = own[...]
    for node in range(supernodes):
        lanes = slice(node * width, (node + 1) * width)
        value = packed(panels_far, node, low, parity) * keep_far[:, node : node + 1]
        block[1 - parity, :, lanes] = value.astype(jnp.bfloat16)


def merge_kernel(block, block_core, near, near_core, chip, first, second):
    carry = lax.axis_index("pcol") == 0
    _, rows_half, _ = block.shape
    for core, source in ((0, block_core), (1, block)):
        for x in range(2):
            rows = slice(x * rows_half, (x + 1) * rows_half)
            chip[core, rows] = source[x]
            first[core, rows] = jnp.where(carry, near[core, rows], source[x])
            second[core, rows] = jnp.where(carry, near_core[core, rows], source[x])


def product_kernel(near, near_core, far_0, far_1, held, out):
    count, _, rows_dev, lanes = held.shape
    depth = count * rows_dev
    for core, lefts in ((0, (near_core, far_0)), (1, (near, far_1))):
        right = held[:, core].reshape(depth, lanes)
        for far_or, left in enumerate(lefts):
            value = jnp.dot(left[...].reshape(2 * rows_dev, depth), right, preferred_element_type=jnp.float32)
            value = value.reshape(out.shape[1:])
            out[far_or] = value if core == 0 else out[far_or] + value


def left_kernel(panels, panels_far, panels_core, panels_far_core, out, rows):
    supernodes, _, rows_half, width = panels.shape
    for node in range(supernodes):
        for part in range(2):
            for far_or, (same, cross) in ((0, (panels, panels_core)), (1, (panels_far, panels_far_core))):
                rows[far_or, 0] = cross[node, part]
                rows[far_or, 1] = same[node, part]
            out[node, part] = rows[...].reshape(4 * rows_half, width).T


def columns_and_diagonal(orders, head, value_of, kept, left, own, send, diag, columns):
    supernodes, rows_half, width = own.shape
    rows_dev = 2 * rows_half
    some = supernodes * rows_half
    peaks = []
    for far_or in range(2):
        real, imag = value_of(far_or)
        for node in range(supernodes):
            lanes = slice(node * width, (node + 1) * width)
            keep = kept[far_or, :, node : node + 1]
            column = (-((real[:, lanes] + turned(imag[:, lanes])) * keep)).astype(jnp.bfloat16)
            columns[node, far_or] = column
            if far_or == 0:
                send[node * rows_half : (node + 1) * rows_half] = column[:rows_half]
                own[node] = column[rows_half:]
            else:
                peaks.append(jnp.abs(column.astype(jnp.float32)))
    level = level_of(largest(functools.reduce(jnp.maximum, peaks)), 13)
    factor = power(level, 0, STEP)
    send[3 * some :] = jnp.broadcast_to(level, (LEVEL_ROWS, width)).astype(jnp.bfloat16)
    for node in range(supernodes):
        column = (columns[node, 1].astype(jnp.float32) * factor).astype(jnp.bfloat16)
        start = some + node * rows_half
        send[start : start + rows_half] = column[:rows_half]
        send[start + some : start + some + rows_half] = column[rows_half:]
    values = []
    for node in range(supernodes):
        both = jnp.dot(
            left[node].reshape(2 * width, 2 * rows_dev),
            columns[node].reshape(2 * rows_dev, width),
            preferred_element_type=jnp.float32,
        )
        values.append(both[:width] + turned(both[width:]))
    for node, value in enumerate(values):
        diag[node * width : (node + 1) * width] = value
    level = level_of(largest(functools.reduce(jnp.maximum, [jnp.abs(value) for value in values])), head + orders)
    diag[supernodes * width :] = jnp.broadcast_to(level, (LEVEL_ROWS, width))


def diagonal_kernel(orders, head, product, *refs):
    columns_and_diagonal(orders, head, lambda far_or: (product[far_or, 0], product[far_or, 1]), *refs)


def whole_kernel(orders, head, near, near_core, far_0, far_1, block_0, block_1, block_2, block_3, *refs):
    _, rows_dev, depth = near.shape
    blocks = (block_0, block_1, block_2, block_3)
    right = jnp.concatenate([block[core] for core in range(2) for block in blocks])

    def value_of(far_or):
        pair = ((near_core, near), (far_0, far_1))[far_or]
        both = jnp.concatenate([part[...].reshape(2 * rows_dev, depth) for part in pair], axis=1)
        value = jnp.dot(both, right, preferred_element_type=jnp.float32)
        return value[:rows_dev], value[rows_dev:]

    columns_and_diagonal(orders, head, value_of, *refs)


def unpack(near, far):
    parity = lax.axis_index("prow") % 2
    low = jnp.where(parity == 0, near, far)
    high = jnp.where(parity == 0, far, near)
    first = lax.broadcasted_iota(jnp.int32, near.shape, 1) < near.shape[1] // 2
    return jnp.where(first, low, swap_halves(high)), jnp.where(first, swap_halves(low), high)


def columns_kernel(own, own_core, other, other_core, out):
    supernodes, _, rows_half, width = out.shape
    first = lax.axis_index("pcol") == 0
    for node in range(supernodes):
        rows = slice(node * rows_half, (node + 1) * rows_half)
        near = jnp.where(first, own_core[rows].astype(jnp.float32), own[rows].astype(jnp.float32))
        far = jnp.where(first, other[rows].astype(jnp.float32), other_core[rows].astype(jnp.float32))
        real, imag = unpack(near, far)
        out[node, 0] = real.astype(jnp.bfloat16)
        out[node, 1] = imag.astype(jnp.bfloat16)


def final_kernel(orders, diag_inverse, mine, far, mine_core, far_core, out, value, done):
    supernodes, _, width, _ = out.shape
    first = lax.axis_index("pcol") == 0
    end = supernodes * width
    near_level = jnp.where(first, mine_core[end : end + 1], mine[end : end + 1])
    far_level = jnp.where(first, far_core[end : end + 1], far[end : end + 1])
    near_scale, far_scale = power(near_level, orders, -STEP), power(far_level, orders, -STEP)
    copies = [pltpu.make_async_copy(value.at[node], out.at[node], done.at[node]) for node in range(supernodes)]
    for node in range(supernodes):
        rows = slice(node * width, (node + 1) * width)
        near_value = jnp.where(first, mine_core[rows], mine[rows]) * near_scale
        far_value = jnp.where(first, far_core[rows], far[rows]) * far_scale
        real, imag = unpack(near_value, far_value)
        value[node, 0] = diag_inverse[node, 0].astype(jnp.float32) - real
        value[node, 1] = diag_inverse[node, 1].astype(jnp.float32) - imag
        copies[node].start()
    for copy in copies:
        copy.wait()


def solution(mesh):
    rows, cols = mesh.shape["prow"], mesh.shape["pcol"]

    def local(anc_inverse, panels, diag_inverse, structure):
        supernodes, _, rows_half, width = panels.shape
        half = width // 2
        groups = anc_inverse.shape[1]
        rows_dev = anc_inverse.shape[4]
        lanes = supernodes * width
        row_index = lax.axis_index("prow")
        col_index = lax.axis_index("pcol")
        here = row_index // 2
        bf16, f32 = jnp.bfloat16, jnp.float32

        panels = plain(panels)
        panels_far = plain(swap(panels, rows, cols, 1, 1))
        chip_shape = (2, rows_dev, lanes)
        shape = (2, rows_dev, groups * rows_half)
        near, panels, diag_inverse, keep, keep_far, own = call(
            first_kernel,
            [
                (shape, bf16),
                (panels.shape, bf16),
                (diag_inverse.shape, bf16),
                ((2, rows_dev, 128), f32),
                ((rows_half, 128), f32),
                ((rows_half, lanes), bf16),
            ],
            [pltpu.with_memory_space_constraint(v, pltpu.HBM) for v in (anc_inverse, panels, diag_inverse, structure)],
            [
                pltpu.VMEM(anc_inverse.shape, bf16),
                pltpu.VMEM(structure.shape, jnp.int32),
                pltpu.SemaphoreType.DMA((4,)),
            ],
            cost=12 << 20,
            space=HBM,
        )
        near_core = swap_core(near)
        panels_core = swap_core(panels)
        (block,) = call(pick_kernel, [((2, rows_half, lanes), bf16)], [own, keep_far, panels_far])
        if shape == chip_shape:
            chip, first, second = call(
                merge_kernel, [(chip_shape, bf16)] * 3, [block, swap_core(block), near, near_core]
            )
            far_0 = far_1 = None
        else:
            chip = first = second = jnp.stack([swap_core(block), block]).reshape(chip_shape)
            far_1 = swap(near, rows, cols, 1, 1)
            far_0 = swap_core(far_1)
        arrived = [swap(value, rows, cols, 1, mask) for value, mask in zip((first, second, chip), MASKS)]
        if far_0 is None:
            far_0, far_1 = swap_core(arrived[0]), swap_core(arrived[1])
        panels_far_core = swap_core(panels_far)
        (left,) = call(
            left_kernel,
            [((supernodes, 2, width, 2 * rows_dev), bf16)],
            [panels, panels_far, panels_core, panels_far_core],
            [pltpu.VMEM((2, cols, rows_half, width), bf16)],
        )
        orders = max(0, math.ceil(math.log2(groups * 2 * rows_half / 24)))
        head = 15 - int(math.log2(rows // 2))
        count = supernodes * width
        some = supernodes * rows_half
        outs = [
            ((supernodes, rows_half, width), bf16),
            ((3 * some + LEVEL_ROWS, width), bf16),
            ((count + LEVEL_ROWS, width), f32),
        ]
        sums = (2, 2, rows_dev, lanes)
        columns_scratch = pltpu.VMEM((supernodes, 2, rows_dev, width), bf16)
        lefts = [near, near_core, far_0, far_1]
        arrived = list(lax.optimization_barrier(tuple(arrived)))
        if rows == 8:
            own, send, diag = call(
                functools.partial(whole_kernel, orders, head),
                outs,
                lefts + [chip] + arrived + [keep, left],
                [columns_scratch],
            )
        else:
            held = jnp.stack([chip] + arrived)
            size = 8
            while size < rows:
                held = jnp.concatenate([held, swap(held, rows, cols, 1, size)])
                size *= 2
            (product,) = call(product_kernel, [(sums, f32)], lefts + [held])
            own, send, diag = call(
                functools.partial(diagonal_kernel, orders, head), outs, [product, keep, left], [columns_scratch]
            )
        f16 = jnp.float16
        is_level = lax.broadcasted_iota(jnp.int32, diag.shape, 0) >= count
        level = diag[count : count + 1]
        term = jnp.where(is_level, level, diag * power(level, -orders, STEP)).astype(f16)
        sent = swap_core(send)
        last = jnp.concatenate([sent[some:].astype(f16), term[2 * some + LEVEL_ROWS :]])
        last = jnp.where(col_index == 0, last, term)
        terms = [swap(v, rows, cols, 1, mask) for mask, v in zip(MASKS_SUM, (term, term, last))]
        wide = [t.astype(f32) for t in [term] + terms]
        levels = [t[count : count + 1] for t in wide]
        mine, first, second, third = [t * power(v, orders, -STEP) for t, v in zip(wide, levels)]
        total = (mine + first) + (second + third)
        level = functools.reduce(jnp.minimum, levels)
        size = 8
        while size < rows:
            other = swap(jnp.where(is_level, level, total), rows, cols, 1, size)
            total, level = total + other, jnp.minimum(level, other[count : count + 1])
            size *= 2
        mine = jnp.where(is_level, level, total * power(level, -orders, STEP)).astype(f16)
        far = swap(mine, rows, cols, 2, 1)
        other = wide[3][: 2 * some] * power(wide[3][2 * some : 2 * some + 1], 0, -STEP)
        other = other.astype(bf16)
        (columns,) = call(
            columns_kernel,
            [((supernodes, 2, rows_half, width), bf16)],
            [own.reshape(some, width), sent[:some], other[:some], swap_core(other[some:])],
        )
        far_sent = far
        far_sent = after(far, columns)
        pieces = [v.astype(f32) for v in (mine, far, swap_core(mine), swap_core(far_sent))]
        (diag,) = call(
            functools.partial(final_kernel, orders),
            [((supernodes, 2, width, width), f32)],
            [diag_inverse] + pieces,
            [pltpu.VMEM((supernodes, 2, width, width), f32), pltpu.SemaphoreType.DMA((supernodes,))],
            out_space=HBM,
        )
        return columns, diag

    in_specs = (
        P("pole", None, "pcol", None, "prow"),
        P("pole", None, ("prow", "pcol"), None),
        P("pole", None, None, None),
        P(),
    )
    out_specs = (P("pole", None, ("prow", "pcol"), None), P("pole", None, None, None))
    return jax.shard_map(local, mesh=mesh, in_specs=in_specs, out_specs=out_specs, check_vma=False)
```
